32 devices in a mesh: group: 4 (over y, core), blk: 4 (over z), mp: 2 (over x).
Axes of the slice: x: 2, y: 2, z: 4, core: 2. Of those that a mesh axis runs over, the one named last changes fastest.
Arguments:
- image_hidden: bfloat16 [1024, 1408], P('blk', 'mp'), may hold values from -6 to 6
- image_weight: bfloat16 [1408, 1536], P('mp'), may hold values from -0.00390625 to 0.00390625
- text_embed: bfloat16 [1024, 1536], P(('group', 'blk', 'mp')), may hold values from -0.19921875 to 0.19921875
- positives: int32 [1024], P('blk'), may hold values from 0 to 1023, each once
- log_temp: float32 [1], replicated, may hold values from 1.6 to 3
- bias: float32 [1], replicated, may hold values from -10 to -5
Outputs:
- loss: float32 [1], replicated
- grad_temp: float32 [1], replicated
- grad_bias: float32 [1], replicated
- grad_image: float32 [1024, 1536], P('blk')
- grad_text: float32 [1024, 1536], P(('group', 'blk', 'mp'))
- grad_weight: float32 [1408, 1536], P('mp', ('group', 'blk'))
The draws below stay inside these ranges and needn't reach their ends.
Inputs may be any that keep to these rules, and one draw needn't show every extreme that they name: positives is a permutation: every text is the positive of exactly one image.
All inputs are finite; a program needn't handle non-finite values.
Results may differ from the reference program's by a relative error of at most 0.0045.
Values may be sent and summed in bfloat16 or wider, within the bound.
A program may use at most 64 MiB of HBM per device.

```python
import jax
import jax.numpy as jnp
from jax import lax

H = 1408
E = 1536
PAIRS = 1024


def steps_of(key, dims, pieces, least, top_value):
    level = 1.0
    for dim, shards_of in pieces:
        steps = jax.random.uniform(jax.random.fold_in(jax.random.fold_in(key, 6), dim), (shards_of,), jnp.float32, least / len(pieces), top_value / len(pieces))
        level = level * jnp.repeat(jnp.exp(steps), dims[dim] // shards_of).reshape((-1,) + (1,) * (len(dims) - 1 - dim))
    return level


def gaussian(own_key, dims, scale, most, cuts=(), kind=jnp.bfloat16):
    entries = scale * jax.random.normal(own_key, dims, jnp.float32)
    if cuts:
        entries = entries * steps_of(own_key, dims, cuts, -0.22, 0.18)
    return jnp.clip(entries, -most, most).astype(kind)


def setup_inputs(seed: int = 0) -> dict:
    keys = jax.random.split(jax.random.key(seed), 7)
    image_hidden = gaussian(keys[0], (PAIRS, H), 1.0, 6.0, ((0, 4), (1, 2)))
    image_weight = gaussian(keys[1], (H, E), (H * E) ** -0.5, 0.00390625, ((0, 2),))
    text_embed = gaussian(keys[2], (PAIRS, E), 0.03, 0.19921875, ((0, 32),))
    positives = jax.random.permutation(keys[3], PAIRS).astype(jnp.int32)
    log_temp = jnp.clip(jax.random.uniform(keys[4], (1,), jnp.float32, 1.6, 3.0), 1.6, 3.0)
    bias = jnp.clip(jax.random.uniform(keys[5], (1,), jnp.float32, -10.0, -5.0), -10.0, -5.0)
    return dict(image_hidden=image_hidden, image_weight=image_weight, text_embed=text_embed, positives=positives, log_temp=log_temp, bias=bias)


def unit_rows(values):
    norm_rows = jnp.sqrt(lax.optimization_barrier(jnp.sum(values * values, axis=1, keepdims=True)) + 1e-06)
    return (values / norm_rows, norm_rows)

def unit_backward(grads, unit, norm_rows):
    return (grads - unit * lax.optimization_barrier(jnp.sum(unit * grads, axis=1, keepdims=True))) / norm_rows

def reference(image_hidden, image_weight, text_embed, positives, log_temp, bias):
    image_emb = jnp.dot(image_hidden, image_weight, preferred_element_type=jnp.float32)
    image_unit, image_norm = unit_rows(image_emb)
    image_low = image_unit.astype(jnp.bfloat16)
    text_unit, text_norm = unit_rows(text_embed.astype(jnp.float32))
    text_low = text_unit.astype(jnp.bfloat16)
    scale = jnp.exp(log_temp[0])
    sims = jnp.dot(image_low, text_low.T, preferred_element_type=jnp.float32)
    logits = scale * sims + bias[0]
    column = jnp.arange(PAIRS, dtype=jnp.int32)
    signs = jnp.where(column[None, :] == positives[:, None], 1.0, -1.0).astype(jnp.float32)
    loss = -jnp.sum(jax.nn.log_sigmoid(signs * logits)) / PAIRS
    slopes = -signs * jax.nn.sigmoid(-signs * logits)
    grad_temp = scale * jnp.sum(slopes * sims) / PAIRS
    grad_bias = jnp.sum(slopes) / PAIRS
    weights = (scale * slopes).astype(jnp.bfloat16)
    grad_unit_image = jnp.dot(weights, text_low, preferred_element_type=jnp.float32)
    grad_unit_text = jnp.dot(weights.T, image_low, preferred_element_type=jnp.float32)
    grad_image = unit_backward(grad_unit_image, image_unit, image_norm)
    grad_text = unit_backward(grad_unit_text, text_unit, text_norm)
    grad_weight = jnp.dot(image_hidden.T, grad_image.astype(jnp.bfloat16), preferred_element_type=jnp.float32)
    return (loss.reshape(1), grad_temp.reshape(1), grad_bias.reshape(1), grad_image, grad_text, grad_weight)
```

```python
import functools

import jax
import jax.numpy as jnp
from jax import lax
from jax.experimental import pallas as pl
from jax.experimental.pallas import tpu as pltpu
from jax.sharding import PartitionSpec as P

MESH = pl.DeviceIdType.MESH
LANES = 128
F32 = jnp.float32
BF16 = jnp.bfloat16


def row_norm(values):
    return jnp.sqrt(jnp.sum(values * values, axis=1, keepdims=True) + 1e-06)


def unit_backward(grads, unit, norm_rows):
    return (grads - unit * jnp.sum(unit * grads, axis=1, keepdims=True)) / norm_rows


def kernel(
    sizes,
    hid_ref, w_ref, txt_ref, pos_ref, temp_ref, bias_ref,
    loss_ref, gtemp_ref, gbias_ref, gimg_ref, gtxt_ref, gw_ref,
    part_recv, own_part, unit_ref, norm_ref, img, txt, hid_all,
    wts, gi_send, gi_recv, gi_own, low, gt_send, gt_recv, gt_own,
    col_send, col_recv, stat_plane, stat_all, total,
    part_s, part_r, img_s, img_r, txt_s, txt_r, hid_s, hid_r, gi_s, gi_r,
    low_s, low_r, gt_s, gt_r, col_s, col_r, sp_s, sp_r, sa_s, sa_r,
):
    groups, blocks, splits = sizes
    plane = groups * splits
    rows, emb = img.shape
    own = rows // plane
    texts = txt_ref.shape[0]
    pairs = rows * blocks
    group_cols = emb // groups
    cols = group_cols // blocks
    chunk = group_cols
    g, z, x = lax.axis_index("group"), lax.axis_index("blk"), lax.axis_index("mp")
    p = g * splits + x

    def in_plane(k):
        q = lax.rem(p + k, plane)
        return q, (lax.div(q, splits), z, lax.rem(q, splits))

    def from_plane(k):
        return lax.rem(p + plane - k, plane)

    def along(k):
        q = lax.rem(z + k, blocks)
        return q, (g, q, x)

    def from_along(k):
        return lax.rem(z + blocks - k, blocks)

    def slot(i, size):
        return pl.ds(pl.multiple_of(i * size, size), size)

    def copy(src, dst, send_sem, recv_sem, device):
        return pltpu.make_async_remote_copy(
            src_ref=src, dst_ref=dst, send_sem=send_sem, recv_sem=recv_sem,
            device_id=device, device_id_type=MESH,
        )

    sent = []

    def send(*args):
        c = copy(*args)
        c.start()
        sent.append(c)

    def landed(dst, send_sem, recv_sem, device):
        copy(dst, dst, send_sem, recv_sem, device).wait_recv()

    barrier = pltpu.get_barrier_semaphore()
    for k in range(1, plane):
        pl.semaphore_signal(barrier, inc=1, device_id=in_plane(k)[1], device_id_type=MESH)
    for k in range(1, blocks):
        pl.semaphore_signal(barrier, inc=1, device_id=along(k)[1], device_id_type=MESH)

    text = txt_ref[...].astype(F32)
    txt[slot(z, texts), :] = (text / row_norm(text)).astype(BF16)
    mine = hid_ref[slot(g, splits * own), :]
    for j in range(emb // chunk):
        at = slice(j * chunk, (j + 1) * chunk)
        own_part[:, at] = jnp.dot(mine, w_ref[:, at], preferred_element_type=F32)
    pl.semaphore_wait(barrier, plane - 1 + blocks - 1)

    for k in range(1, splits):
        q = lax.rem(x + k, splits)
        send(own_part.at[slot(q, own), :], part_recv.at[slot(x, own), :],
             part_s.at[k], part_r.at[k], (g, z, q))
    for k in range(1, blocks):
        here = txt.at[slot(z, texts), :]
        send(here, here, txt_s.at[k], txt_r.at[k], along(k)[1])

    emb_rows = own_part[slot(x, own), :]
    for k in range(1, splits):
        q = lax.rem(x + splits - k, splits)
        there = part_recv.at[slot(q, own), :]
        landed(there, part_s.at[k], part_r.at[k], (g, z, q))
        emb_rows = emb_rows + there[...]
    norm = row_norm(emb_rows)
    unit = emb_rows / norm
    unit_ref[...] = unit
    norm_ref[...] = jnp.broadcast_to(norm, norm_ref.shape)
    img[slot(p, own), :] = unit.astype(BF16)
    for k in range(1, plane):
        here = img.at[slot(p, own), :]
        send(here, here, img_s.at[k], img_r.at[k], in_plane(k)[1])

    for k in range(1, blocks):
        there = txt.at[slot(from_along(k), texts), :]
        landed(there, txt_s.at[k], txt_r.at[k], along(k)[1])
    for k in range(1, blocks):
        send(hid_ref, hid_all.at[z], hid_s.at[k], hid_r.at[k], along(k)[1])
    hid_all[z] = hid_ref[...]
    for k in range(1, plane):
        there = img.at[slot(from_plane(k), own), :]
        landed(there, img_s.at[k], img_r.at[k], in_plane(k)[1])

    count = blocks * texts
    sims = lax.dot_general(
        img[...], txt[...], (((1,), (1,)), ((), ())), preferred_element_type=F32
    )
    scale = jnp.exp(temp_ref[...])
    logits = scale * sims + bias_ref[...]
    at = lax.broadcasted_iota(jnp.int32, (1, count), 1)
    column = at + (g * blocks * splits + x) * texts
    for j in range(1, blocks):
        column = column + jnp.where(at >= j * texts, (splits - 1) * texts, 0)
    match = column == pos_ref[...]
    signed = jnp.where(match, logits, -logits)
    small = jnp.exp(-jnp.abs(signed))
    loss_at = jnp.log1p(small) - jnp.minimum(signed, 0.0)
    slope = jnp.where(signed >= 0.0, small, 1.0) / (1.0 + small)
    slope = jnp.where(match, -slope, slope)
    weights = (scale * slope).astype(BF16)
    wts[...] = weights

    for j in range(emb // chunk):
        c = slice(j * chunk, (j + 1) * chunk)
        value = jnp.dot(wts[...], txt[:, c], preferred_element_type=F32)
        gi_send[:, c] = value.astype(BF16)
        gi_own[:, c] = value
    for k in range(1, plane):
        q, device = in_plane(k)
        send(gi_send.at[slot(q, own), :], gi_recv.at[slot(p, own), :],
             gi_s.at[k], gi_r.at[k], device)

    def add_all(v):
        return jnp.sum(jnp.sum(v, axis=1, keepdims=True), axis=0, keepdims=True)

    line = lax.broadcasted_iota(jnp.int32, (8, LANES), 0)
    stat = jnp.where(line == 0, add_all(loss_at), 0.0)
    stat = jnp.where(line == 1, add_all(slope * sims), stat)
    stat = jnp.where(line == 2, add_all(slope), stat)
    stat_plane[p] = stat
    for k in range(1, plane):
        here = stat_plane.at[p]
        send(here, here, sp_s.at[k], sp_r.at[k], in_plane(k)[1])

    for j in range(emb // chunk):
        c = slice(j * chunk, (j + 1) * chunk)
        value = lax.dot_general(
            wts[...], img[:, c], (((0,), (0,)), ((), ())), preferred_element_type=F32
        )
        gt_send[:, c] = value.astype(BF16)
        gt_own[:, c] = value
    for k in range(1, blocks):
        q, device = along(k)
        send(gt_send.at[slot(q, texts), :], gt_recv.at[slot(z, texts), :],
             gt_s.at[k], gt_r.at[k], device)

    grads = gi_own[slot(p, own), :]
    for k in range(1, plane):
        there = gi_recv.at[slot(from_plane(k), own), :]
        landed(there, gi_s.at[k], gi_r.at[k], in_plane(k)[1])
        grads = grads + there[...].astype(F32)
    low[slot(p, own), :] = unit_backward(grads, unit_ref[...], norm_ref[:, :1]).astype(BF16)
    for k in range(1, plane):
        here = low.at[slot(p, own), :]
        send(here, here, low_s.at[k], low_r.at[k], in_plane(k)[1])

    for k in range(1, plane):
        there = stat_plane.at[from_plane(k)]
        landed(there, sp_s.at[k], sp_r.at[k], in_plane(k)[1])
    stat = stat_plane[0]
    for j in range(1, plane):
        stat = stat + stat_plane[j]
    stat_all[z] = stat
    for k in range(1, blocks):
        here = stat_all.at[z]
        send(here, here, sa_s.at[k], sa_r.at[k], along(k)[1])

    grads = gt_own[slot(z, texts), :]
    for k in range(1, blocks):
        there = gt_recv.at[slot(from_along(k), texts), :]
        landed(there, gt_s.at[k], gt_r.at[k], along(k)[1])
        grads = grads + there[...].astype(F32)
    text = txt_ref[...].astype(F32)
    norm = row_norm(text)
    gtxt_ref[...] = unit_backward(grads, text / norm, norm)

    for k in range(1, blocks):
        there = stat_all.at[from_along(k)]
        landed(there, sa_s.at[k], sa_r.at[k], along(k)[1])
    stat = stat_all[0]
    for j in range(1, blocks):
        stat = stat + stat_all[j]
    loss_ref[...] = stat[0:1, 0:1] / pairs
    gtemp_ref[...] = scale * stat[1:2, 0:1] / pairs
    gbias_ref[...] = stat[2:3, 0:1] / pairs

    for k in range(1, plane):
        there = low.at[slot(from_plane(k), own), :]
        landed(there, low_s.at[k], low_r.at[k], in_plane(k)[1])
    wide = low[:, slot(g, group_cols)]
    for j in range(blocks):
        col_send[j, :, 0:cols] = wide[:, j * cols:(j + 1) * cols]
    for k in range(1, blocks):
        q, device = along(k)
        send(col_send.at[q], col_recv.at[z], col_s.at[k], col_r.at[k], device)
    gimg_ref[...] = low[...]
    col_recv[z] = col_send[z]
    for k in range(1, blocks):
        landed(hid_all.at[from_along(k)], hid_s.at[k], hid_r.at[k], along(k)[1])
    total[...] = jnp.zeros_like(total)
    for k in range(blocks):
        q = from_along(k)
        if k:
            landed(col_recv.at[q], col_s.at[k], col_r.at[k], along(k)[1])
        total[...] += lax.dot_general(
            hid_all[q], col_recv[q], (((0,), (0,)), ((), ())), preferred_element_type=F32
        )
    gw_ref[...] = total[:, 0:cols]
    for c in sent:
        c.wait_send()


def on_device(image_hidden, image_weight, text_embed, positives, log_temp, bias):
    groups, blocks, splits = (lax.axis_size(a) for a in ("group", "blk", "mp"))
    plane = groups * splits
    rows, depth = image_hidden.shape
    emb = image_weight.shape[1]
    texts = text_embed.shape[0]
    own = rows // plane
    count = blocks * texts
    cols = emb // (groups * blocks)
    width = -(-cols // LANES) * LANES
    vmem = pl.BlockSpec(memory_space=pltpu.VMEM)
    dma = pltpu.SemaphoreType.DMA
    outs = pl.pallas_call(
        functools.partial(kernel, (groups, blocks, splits)),
        out_shape=[
            jax.ShapeDtypeStruct((1, 1), F32),
            jax.ShapeDtypeStruct((1, 1), F32),
            jax.ShapeDtypeStruct((1, 1), F32),
            jax.ShapeDtypeStruct((rows, emb), BF16),
            jax.ShapeDtypeStruct((texts, emb), F32),
            jax.ShapeDtypeStruct((depth, cols), F32),
        ],
        in_specs=[vmem] * 6,
        out_specs=[vmem] * 6,
        scratch_shapes=[
            pltpu.VMEM((splits * own, emb), F32),
            pltpu.VMEM((splits * own, emb), F32),
            pltpu.VMEM((own, emb), F32),
            pltpu.VMEM((own, LANES), F32),
            pltpu.VMEM((rows, emb), BF16),
            pltpu.VMEM((count, emb), BF16),
            pltpu.VMEM((blocks, rows, depth), BF16),
            pltpu.VMEM((rows, count), BF16),
            pltpu.VMEM((rows, emb), BF16),
            pltpu.VMEM((rows, emb), BF16),
            pltpu.VMEM((rows, emb), F32),
            pltpu.VMEM((rows, emb), BF16),
            pltpu.VMEM((count, emb), BF16),
            pltpu.VMEM((count, emb), BF16),
            pltpu.VMEM((count, emb), F32),
            pltpu.VMEM((blocks, rows, width), BF16),
            pltpu.VMEM((blocks, rows, width), BF16),
            pltpu.VMEM((plane, 8, LANES), F32),
            pltpu.VMEM((blocks, 8, LANES), F32),
            pltpu.VMEM((depth, width), F32),
            dma((splits,)), dma((splits,)),
            dma((plane,)), dma((plane,)),
            dma((blocks,)), dma((blocks,)),
            dma((blocks,)), dma((blocks,)),
            dma((plane,)), dma((plane,)),
            dma((plane,)), dma((plane,)),
            dma((blocks,)), dma((blocks,)),
            dma((blocks,)), dma((blocks,)),
            dma((plane,)), dma((plane,)),
            dma((blocks,)), dma((blocks,)),
        ],
        compiler_params=pltpu.CompilerParams(
            collective_id=0, has_side_effects=True, vmem_limit_bytes=50 * 1024 * 1024
        ),
        name="contrast",
    )(
        image_hidden, image_weight, text_embed, positives.reshape(rows, 1),
        log_temp.reshape(1, 1), bias.reshape(1, 1),
    )
    loss, grad_temp, grad_bias, grad_image, grad_text, grad_weight = outs
    return (
        loss.reshape(1), grad_temp.reshape(1), grad_bias.reshape(1),
        grad_image.astype(F32), grad_text, grad_weight,
    )


def solution(mesh):
    in_specs = (P("blk", "mp"), P("mp", None), P(("group", "blk", "mp"), None), P("blk"), P(), P())
    out_specs = (
        P(),
        P(),
        P(),
        P("blk", None),
        P(("group", "blk", "mp"), None),
        P("mp", ("group", "blk")),
    )
    return jax.shard_map(
        on_device, mesh=mesh, in_specs=in_specs, out_specs=out_specs, check_vma=False
    )
```

```python
import functools

import jax
import jax.numpy as jnp
from jax import lax
from jax.experimental import pallas as pl
from jax.experimental.pallas import tpu as pltpu
from jax.sharding import PartitionSpec as P

MESH = pl.DeviceIdType.MESH
LANES = 128
F32 = jnp.float32
BF16 = jnp.bfloat16


def row_norm(values):
    return jnp.sqrt(jnp.sum(values * values, axis=1, keepdims=True) + 1e-06)


def unit_backward(grads, unit, norm_rows):
    return (grads - unit * jnp.sum(unit * grads, axis=1, keepdims=True)) / norm_rows


def kernel(
    sizes,
    hid_ref, w_ref, txt_ref, pos_ref, temp_ref, bias_ref,
    loss_ref, gtemp_ref, gbias_ref, gimg_ref, gtxt_ref, gw_ref,
    part_recv, own_part, unit_ref, norm_ref, img, txt, hid_all,
    wts, gi_own, gi_pair, gi_send, gi_recv, low, gt_send, gt_recv, gt_own,
    col_send, col_mid, col_all, stat_plane, stat_all, total,
    part_s, part_r, img_s, img_r, txt_s, txt_r, hid_s, hid_r, gp_s, gp_r, gi_s, gi_r,
    low_s, low_r, gt_s, gt_r, cz_s, cz_r, cp_s, cp_r, sp_s, sp_r, sa_s, sa_r,
):
    groups, blocks, splits = sizes
    plane = groups * splits
    pair = 2 if groups % 2 == 0 else 1
    outer = groups // pair
    chips = outer * splits
    rows, emb = img.shape
    own = rows // plane
    band = splits * own
    texts = txt_ref.shape[0]
    pairs = rows * blocks
    group_cols = emb // groups
    cols = group_cols // blocks
    width = total.shape[0]
    part_rows = rows // pair
    chunk = group_cols
    g, z, x = lax.axis_index("group"), lax.axis_index("blk"), lax.axis_index("mp")
    p = g * splits + x
    half, out = lax.rem(g, pair), lax.div(g, pair)
    chip = out * splits + x
    sibling = (out * pair + (pair - 1 - half), z, x)

    def in_plane(k):
        q = lax.rem(p + k, plane)
        return q, (lax.div(q, splits), z, lax.rem(q, splits))

    def from_plane(k):
        return lax.rem(p + plane - k, plane)

    def on_chip(c, h):
        return (lax.div(c, splits) * pair + h) * splits + lax.rem(c, splits)

    def chip_device(c):
        return (lax.div(c, splits) * pair + half, z, lax.rem(c, splits))

    def to_chip(k):
        return lax.rem(chip + k, chips)

    def from_chip(k):
        return lax.rem(chip + chips - k, chips)

    def along(k):
        q = lax.rem(z + k, blocks)
        return q, (g, q, x)

    def from_along(k):
        return lax.rem(z + blocks - k, blocks)

    def slot(i, size):
        return pl.ds(pl.multiple_of(i * size, size), size)

    def copy(src, dst, send_sem, recv_sem, device):
        return pltpu.make_async_remote_copy(
            src_ref=src, dst_ref=dst, send_sem=send_sem, recv_sem=recv_sem,
            device_id=device, device_id_type=MESH,
        )

    sent = []

    def send(*args):
        c = copy(*args)
        c.start()
        sent.append(c)

    def landed(dst, send_sem, recv_sem, device):
        copy(dst, dst, send_sem, recv_sem, device).wait_recv()

    def gather_start(buf, s_sem, r_sem):
        here = buf.at[slot(p, own), :]
        for k in range(1, chips):
            send(here, here, s_sem.at[k], r_sem.at[k], chip_device(to_chip(k)))
        if pair == 2:
            send(here, here, s_sem.at[chips], r_sem.at[chips], sibling)

    def gather_finish(buf, s_sem, r_sem):
        for k in range(1, chips):
            there = buf.at[slot(on_chip(from_chip(k), half), own), :]
            landed(there, s_sem.at[k], r_sem.at[k], chip_device(from_chip(k)))
            if pair == 2:
                send(there, there, s_sem.at[chips + k], r_sem.at[chips + k], sibling)
        if pair == 2:
            for k in range(chips):
                there = buf.at[slot(on_chip(from_chip(k), 1 - half), own), :]
                landed(there, s_sem.at[chips + k], r_sem.at[chips + k], sibling)

    barrier = pltpu.get_barrier_semaphore()
    for k in range(1, plane):
        pl.semaphore_signal(barrier, inc=1, device_id=in_plane(k)[1], device_id_type=MESH)
    for k in range(1, blocks):
        pl.semaphore_signal(barrier, inc=1, device_id=along(k)[1], device_id_type=MESH)

    text = txt_ref[...].astype(F32)
    txt[slot(z, texts), :] = (text / row_norm(text)).astype(BF16)
    hid_all[z] = hid_ref[...].T
    mine = hid_all[z, slot(g, band), :]
    for j in range(emb // chunk):
        at = slice(j * chunk, (j + 1) * chunk)
        own_part[:, at] = jnp.dot(mine, w_ref[:, at], preferred_element_type=F32)
    pl.semaphore_wait(barrier, plane - 1 + blocks - 1)

    for k in range(1, splits):
        q = lax.rem(x + k, splits)
        send(own_part.at[slot(q, own), :], part_recv.at[slot(x, own), :],
             part_s.at[k], part_r.at[k], (g, z, q))
    for k in range(1, blocks):
        here = txt.at[slot(z, texts), :]
        send(here, here, txt_s.at[k], txt_r.at[k], along(k)[1])

    emb_rows = own_part[slot(x, own), :]
    for k in range(1, splits):
        q = lax.rem(x + splits - k, splits)
        there = part_recv.at[slot(q, own), :]
        landed(there, part_s.at[k], part_r.at[k], (g, z, q))
        emb_rows = emb_rows + there[...]
    norm = row_norm(emb_rows)
    unit = emb_rows / norm
    unit_ref[...] = unit
    norm_ref[...] = jnp.broadcast_to(norm, norm_ref.shape)
    img[slot(p, own), :] = unit.astype(BF16)
    gather_start(img, img_s, img_r)

    for k in range(1, blocks):
        there = txt.at[slot(from_along(k), texts), :]
        landed(there, txt_s.at[k], txt_r.at[k], along(k)[1])
    for k in range(1, blocks):
        here = hid_all.at[z, slot(half, part_rows), :]
        send(here, here, hid_s.at[k], hid_r.at[k], along(k)[1])
    gather_finish(img, img_s, img_r)

    count = blocks * texts
    sims = lax.dot_general(
        txt[...], img[...], (((1,), (1,)), ((), ())), preferred_element_type=F32
    )
    scale = jnp.exp(temp_ref[...])
    logits = scale * sims + bias_ref[...]
    at = lax.broadcasted_iota(jnp.int32, (count, 1), 0)
    column = at + (g * blocks * splits + x) * texts
    for j in range(1, blocks):
        column = column + jnp.where(at >= j * texts, (splits - 1) * texts, 0)
    match = column == pos_ref[...]
    signed = jnp.where(match, logits, -logits)
    small = jnp.exp(-jnp.abs(signed))
    loss_at = jnp.log1p(small) - jnp.minimum(signed, 0.0)
    slope = jnp.where(signed >= 0.0, small, 1.0) / (1.0 + small)
    slope = jnp.where(match, -slope, slope)
    wts[...] = (scale * slope).astype(BF16)

    for j in range(emb // chunk):
        c = slice(j * chunk, (j + 1) * chunk)
        gi_own[:, c] = lax.dot_general(
            wts[...], txt[:, c], (((0,), (0,)), ((), ())), preferred_element_type=F32
        )
    if pair == 2:
        for o in range(outer):
            send(gi_own.at[slot(o * pair + 1 - half, band), :], gi_pair.at[o],
                 gp_s.at[o], gp_r.at[o], sibling)

    for j in range(emb // chunk):
        c = slice(j * chunk, (j + 1) * chunk)
        value = jnp.dot(wts[...], img[:, c], preferred_element_type=F32)
        gt_send[:, c] = value.astype(BF16)
        gt_own[:, c] = value
    for k in range(1, blocks):
        q, device = along(k)
        send(gt_send.at[slot(q, texts), :], gt_recv.at[slot(z, texts), :],
             gt_s.at[k], gt_r.at[k], device)

    for o in range(outer):
        value = gi_own[slot(o * pair + half, band), :]
        if pair == 2:
            landed(gi_pair.at[o], gp_s.at[o], gp_r.at[o], sibling)
            value = value + gi_pair[o]
            gi_pair[o] = value
        gi_send[slot(o, band), :] = value.astype(BF16)
    for k in range(1, chips):
        c = to_chip(k)
        send(gi_send.at[slot(c, own), :], gi_recv.at[slot(chip, own), :],
             gi_s.at[k], gi_r.at[k], chip_device(c))

    def add_all(v):
        return jnp.sum(jnp.sum(v, axis=1, keepdims=True), axis=0, keepdims=True)

    line = lax.broadcasted_iota(jnp.int32, (8, LANES), 0)
    stat = jnp.where(line == 0, add_all(loss_at), 0.0)
    stat = jnp.where(line == 1, add_all(slope * sims), stat)
    stat = jnp.where(line == 2, add_all(slope), stat)
    stat_plane[p] = stat
    for k in range(1, plane):
        here = stat_plane.at[p]
        send(here, here, sp_s.at[k], sp_r.at[k], in_plane(k)[1])

    if pair == 2:
        grads = gi_pair[out, slot(x, own), :]
    else:
        grads = gi_own[slot(p, own), :]
    for k in range(1, chips):
        there = gi_recv.at[slot(from_chip(k), own), :]
        landed(there, gi_s.at[k], gi_r.at[k], chip_device(from_chip(k)))
        grads = grads + there[...].astype(F32)
    rounded = unit_backward(grads, unit_ref[...], norm_ref[:, :1]).astype(BF16)
    low[slot(p, own), :] = rounded
    for j in range(blocks):
        for i in range(groups):
            at = i * group_cols + j * cols
            col_send[j, :, i * width:i * width + cols] = rounded[:, at:at + cols]
    for k in range(1, blocks):
        q, device = along(k)
        send(col_send.at[q], col_mid.at[z], cz_s.at[k], cz_r.at[k], device)
    gather_start(low, low_s, low_r)
    col_mid[z] = col_send[z]

    for k in range(1, plane):
        there = stat_plane.at[from_plane(k)]
        landed(there, sp_s.at[k], sp_r.at[k], in_plane(k)[1])
    stat = stat_plane[0]
    for j in range(1, plane):
        stat = stat + stat_plane[j]
    stat_all[z] = stat
    for k in range(1, blocks):
        here = stat_all.at[z]
        send(here, here, sa_s.at[k], sa_r.at[k], along(k)[1])

    for k in range(1, blocks):
        landed(col_mid.at[from_along(k)], cz_s.at[k], cz_r.at[k], along(k)[1])
    for k in range(1, plane):
        q, device = in_plane(k)
        send(col_mid.at[:, :, slot(lax.div(q, splits), width)],
             col_all.at[:, slot(p, own), :], cp_s.at[k], cp_r.at[k], device)
    col_all[:, slot(p, own), :] = col_mid[:, :, slot(g, width)]
    gather_finish(low, low_s, low_r)
    for k in range(1, blocks):
        there = hid_all.at[from_along(k), slot(half, part_rows), :]
        landed(there, hid_s.at[k], hid_r.at[k], along(k)[1])
        if pair == 2:
            send(there, there, hid_s.at[blocks + k], hid_r.at[blocks + k], sibling)
    gimg_ref[...] = low[...]

    grads = gt_own[slot(z, texts), :]
    for k in range(1, blocks):
        there = gt_recv.at[slot(from_along(k), texts), :]
        landed(there, gt_s.at[k], gt_r.at[k], along(k)[1])
        grads = grads + there[...].astype(F32)
    text = txt_ref[...].astype(F32)
    norm = row_norm(text)
    gtxt_ref[...] = unit_backward(grads, text / norm, norm)

    for k in range(1, blocks):
        there = stat_all.at[from_along(k)]
        landed(there, sa_s.at[k], sa_r.at[k], along(k)[1])
    stat = stat_all[0]
    for j in range(1, blocks):
        stat = stat + stat_all[j]
    loss_ref[...] = stat[0:1, 0:1] / pairs
    gtemp_ref[...] = scale * stat[1:2, 0:1] / pairs
    gbias_ref[...] = stat[2:3, 0:1] / pairs

    if pair == 2:
        for k in range(1, blocks):
            there = hid_all.at[from_along(k), slot(1 - half, part_rows), :]
            landed(there, hid_s.at[blocks + k], hid_r.at[blocks + k], sibling)
    for k in range(1, plane):
        there = col_all.at[:, slot(from_plane(k), own), :]
        landed(there, cp_s.at[k], cp_r.at[k], in_plane(k)[1])
    total[...] = jnp.zeros_like(total)
    for q in range(blocks):
        total[...] += lax.dot_general(
            col_all[q], hid_all[q], (((0,), (0,)), ((), ())), preferred_element_type=F32
        )
    gw_ref[...] = total[0:cols, :]
    for c in sent:
        c.wait_send()


def on_device(image_hidden, image_weight, text_embed, positives, log_temp, bias):
    groups, blocks, splits = (lax.axis_size(a) for a in ("group", "blk", "mp"))
    plane = groups * splits
    rows, depth = image_hidden.shape
    emb = image_weight.shape[1]
    texts = text_embed.shape[0]
    own = rows // plane
    pair = 2 if groups % 2 == 0 else 1
    band = splits * own
    count = blocks * texts
    cols = emb // (groups * blocks)
    width = -(-cols // LANES) * LANES
    vmem = pl.BlockSpec(memory_space=pltpu.VMEM)
    dma = pltpu.SemaphoreType.DMA
    outs = pl.pallas_call(
        functools.partial(kernel, (groups, blocks, splits)),
        out_shape=[
            jax.ShapeDtypeStruct((1, 1), F32),
            jax.ShapeDtypeStruct((1, 1), F32),
            jax.ShapeDtypeStruct((1, 1), F32),
            jax.ShapeDtypeStruct((rows, emb), BF16),
            jax.ShapeDtypeStruct((texts, emb), F32),
            jax.ShapeDtypeStruct((cols, depth), F32),
        ],
        in_specs=[vmem] * 6,
        out_specs=[vmem] * 6,
        scratch_shapes=[
            pltpu.VMEM((band, emb), F32),
            pltpu.VMEM((band, emb), F32),
            pltpu.VMEM((own, emb), F32),
            pltpu.VMEM((own, LANES), F32),
            pltpu.VMEM((rows, emb), BF16),
            pltpu.VMEM((count, emb), BF16),
            pltpu.VMEM((blocks, rows, depth), BF16),
            pltpu.VMEM((count, rows), BF16),
            pltpu.VMEM((rows, emb), F32),
            pltpu.VMEM((rows // pair // band, band, emb), F32),
            pltpu.VMEM((rows // pair, emb), BF16),
            pltpu.VMEM((rows // pair, emb), BF16),
            pltpu.VMEM((rows, emb), BF16),
            pltpu.VMEM((count, emb), BF16),
            pltpu.VMEM((count, emb), BF16),
            pltpu.VMEM((count, emb), F32),
            pltpu.VMEM((blocks, own, groups * width), BF16),
            pltpu.VMEM((blocks, own, groups * width), BF16),
            pltpu.VMEM((blocks, rows, width), BF16),
            pltpu.VMEM((plane, 8, LANES), F32),
            pltpu.VMEM((blocks, 8, LANES), F32),
            pltpu.VMEM((width, depth), F32),
            dma((splits,)), dma((splits,)),
            dma((plane,)), dma((plane,)),
            dma((blocks,)), dma((blocks,)),
            dma((2 * blocks,)), dma((2 * blocks,)),
            dma((groups,)), dma((groups,)),
            dma((plane,)), dma((plane,)),
            dma((plane,)), dma((plane,)),
            dma((blocks,)), dma((blocks,)),
            dma((blocks,)), dma((blocks,)),
            dma((plane,)), dma((plane,)),
            dma((plane,)), dma((plane,)),
            dma((blocks,)), dma((blocks,)),
        ],
        compiler_params=pltpu.CompilerParams(
            collective_id=0, has_side_effects=True, vmem_limit_bytes=50 * 1024 * 1024
        ),
        name="contrast",
    )(
        image_hidden.T, image_weight, text_embed, positives.reshape(1, rows),
        log_temp.reshape(1, 1), bias.reshape(1, 1),
    )
    loss, grad_temp, grad_bias, grad_image, grad_text, grad_weight = outs
    return (
        loss.reshape(1), grad_temp.reshape(1), grad_bias.reshape(1),
        grad_image.astype(F32), grad_text, grad_weight.T,
    )


def solution(mesh):
    in_specs = (P("blk", "mp"), P("mp", None), P(("group", "blk", "mp"), None), P("blk"), P(), P())
    out_specs = (
        P(),
        P(),
        P(),
        P("blk", None),
        P(("group", "blk", "mp"), None),
        P("mp", ("group", "blk")),
    )
    return jax.shard_map(
        on_device, mesh=mesh, in_specs=in_specs, out_specs=out_specs, check_vma=False
    )
```

```python
import functools

import jax
import jax.numpy as jnp
from jax import lax
from jax.experimental import pallas as pl
from jax.experimental.pallas import tpu as pltpu
from jax.sharding import PartitionSpec as P

MESH = pl.DeviceIdType.MESH
LANES = 128
F32 = jnp.float32
BF16 = jnp.bfloat16


def row_norm(values):
    return jnp.sqrt(jnp.sum(values * values, axis=1, keepdims=True) + 1e-06)


def unit_backward(grads, unit, norm_rows):
    return (grads - unit * jnp.sum(unit * grads, axis=1, keepdims=True)) / norm_rows


def kernel(
    sizes,
    hid_hbm, w_hbm, txt_hbm, pos_hbm, temp_ref, bias_ref,
    loss_ref, gtemp_ref, gbias_ref, gimg_ref, gtxt_ref, gw_ref,
    hid_ref, w_ref, txt_ref, pos_ref, part_recv, own_part, unit_ref, norm_ref, img, txt, hid_all,
    wts, gi_own, gi_pair, gi_send, gi_recv, low, gt_send, gt_recv, gt_own,
    col_send, col_mid, col_all, stat_plane, stat_all, total,
    load_s, part_s, part_r, img_s, img_r, txt_s, txt_r, hid_s, hid_r, hp_s, hp_r, gp_s, gp_r, gi_s, gi_r,
    low_s, low_r, gt_s, gt_r, cz_s, cz_r, cp_s, cp_r, sp_s, sp_r, sa_s, sa_r,
):
    groups, blocks, splits = sizes
    plane = groups * splits
    pair = 2 if groups % 2 == 0 else 1
    outer = groups // pair
    chips = outer * splits
    rows, emb = img.shape
    own = rows // plane
    band = splits * own
    texts = txt_ref.shape[0]
    pairs = rows * blocks
    group_cols = emb // groups
    cols = group_cols // blocks
    width = total.shape[0]
    part_rows = rows // pair
    chunk = group_cols
    g, z, x = lax.axis_index("group"), lax.axis_index("blk"), lax.axis_index("mp")
    p = g * splits + x
    half, out = lax.rem(g, pair), lax.div(g, pair)
    chip = out * splits + x
    sibling = (out * pair + (pair - 1 - half), z, x)

    def in_plane(k):
        q = lax.rem(p + k, plane)
        return q, (lax.div(q, splits), z, lax.rem(q, splits))

    def from_plane(k):
        return lax.rem(p + plane - k, plane)

    def on_chip(c, h):
        return (lax.div(c, splits) * pair + h) * splits + lax.rem(c, splits)

    def chip_device(c):
        return (lax.div(c, splits) * pair + half, z, lax.rem(c, splits))

    def to_chip(k):
        return lax.rem(chip + k, chips)

    def from_chip(k):
        return lax.rem(chip + chips - k, chips)

    def along(k):
        q = lax.rem(z + k, blocks)
        return q, (g, q, x)

    def from_along(k):
        return lax.rem(z + blocks - k, blocks)

    def slot(i, size):
        return pl.ds(pl.multiple_of(i * size, size), size)

    def copy(src, dst, send_sem, recv_sem, device):
        return pltpu.make_async_remote_copy(
            src_ref=src, dst_ref=dst, send_sem=send_sem, recv_sem=recv_sem,
            device_id=device, device_id_type=MESH,
        )

    sent = []

    def send(*args):
        c = copy(*args)
        c.start()
        sent.append(c)

    def landed(dst, send_sem, recv_sem, device):
        copy(dst, dst, send_sem, recv_sem, device).wait_recv()

    def gather_start(buf, s_sem, r_sem):
        here = buf.at[slot(p, own), :]
        for k in range(1, chips):
            send(here, here, s_sem.at[k], r_sem.at[k], chip_device(to_chip(k)))
        if pair == 2:
            send(here, here, s_sem.at[chips], r_sem.at[chips], sibling)

    def gather_finish(buf, s_sem, r_sem):
        for k in range(1, chips):
            there = buf.at[slot(on_chip(from_chip(k), half), own), :]
            landed(there, s_sem.at[k], r_sem.at[k], chip_device(from_chip(k)))
            if pair == 2:
                send(there, there, s_sem.at[chips + k], r_sem.at[chips + k], sibling)
        if pair == 2:
            for k in range(chips):
                there = buf.at[slot(on_chip(from_chip(k), 1 - half), own), :]
                landed(there, s_sem.at[chips + k], r_sem.at[chips + k], sibling)

    def line_copies(step, at, s_sem, r_sem):
        up = copy(at(z - step), at(z - step), s_sem.at[step], r_sem.at[step], (g, z + 1, x))
        down = copy(at(z + step), at(z + step), s_sem.at[blocks + step],
                    r_sem.at[blocks + step], (g, z - 1, x))
        return (((z - step >= 0) & (z + 1 < blocks), up),
                ((z + step < blocks) & (z - 1 >= 0), down))

    def line_send(step, at, s_sem, r_sem):
        if step < blocks - 1:
            for held, c in line_copies(step, at, s_sem, r_sem):
                pl.when(held)(c.start)

    def line_sent(at, s_sem, r_sem):
        for step in range(blocks - 1):
            for held, c in line_copies(step, at, s_sem, r_sem):
                pl.when(held)(c.wait_send)

    def line_land(step, at, s_sem, r_sem, then=None):
        if step >= blocks - 1:
            return
        for came, q, i, device in (
            (z - 1 - step >= 0, z - 1 - step, step, (g, z - 1, x)),
            (z + 1 + step < blocks, z + 1 + step, blocks + step, (g, z + 1, x)),
        ):
            @pl.when(came)
            def _():
                landed(at(q), s_sem.at[i], r_sem.at[i], device)
                if then is not None:
                    then(q)

    def text_at(q):
        return txt.at[slot(q, texts), :]

    def hid_at(q):
        return hid_all.at[q, slot(half, part_rows), :]

    def hid_pair(q):
        return copy(hid_at(q), hid_at(q), hp_s.at[q], hp_r.at[q], sibling)

    def hid_land(step):
        line_land(step, hid_at, hid_s, hid_r,
                  (lambda q: hid_pair(q).start()) if pair == 2 else None)

    loads = [
        pltpu.make_async_copy(hid_hbm, hid_ref, load_s.at[0]),
        pltpu.make_async_copy(txt_hbm, txt_ref, load_s.at[1]),
        pltpu.make_async_copy(pos_hbm, pos_ref, load_s.at[2]),
    ]
    for j in range(emb // chunk):
        at = slice(j * chunk, (j + 1) * chunk)
        loads.append(pltpu.make_async_copy(w_hbm.at[:, at], w_ref.at[:, at], load_s.at[3 + j]))
    for c in loads:
        c.start()

    barrier = pltpu.get_barrier_semaphore()
    for k in range(1, plane):
        pl.semaphore_signal(barrier, inc=1, device_id=in_plane(k)[1], device_id_type=MESH)
    for k in range(1, blocks):
        pl.semaphore_signal(barrier, inc=1, device_id=along(k)[1], device_id_type=MESH)

    loads[0].wait()
    hid_all[z] = hid_ref[...].T
    loads[1].wait()
    text = txt_ref[...].astype(F32)
    txt[slot(z, texts), :] = (text / row_norm(text)).astype(BF16)
    pl.semaphore_wait(barrier, plane - 1 + blocks - 1)
    line_send(0, text_at, txt_s, txt_r)
    mine = hid_all[z, slot(g, band), :]
    for j in range(emb // chunk):
        at = slice(j * chunk, (j + 1) * chunk)
        loads[3 + j].wait()
        own_part[:, at] = jnp.dot(mine, w_ref[:, at], preferred_element_type=F32)
        for k in range(1, splits):
            q = lax.rem(x + k, splits)
            send(own_part.at[slot(q, own), at], part_recv.at[slot(x, own), at],
                 part_s.at[j, k], part_r.at[j, k], (g, z, q))
    loads[2].wait()
    line_land(0, text_at, txt_s, txt_r)
    line_send(1, text_at, txt_s, txt_r)

    emb_rows = own_part[slot(x, own), :]
    for k in range(1, splits):
        q = lax.rem(x + splits - k, splits)
        there = part_recv.at[slot(q, own), :]
        for j in range(emb // chunk):
            piece = part_recv.at[slot(q, own), j * chunk:(j + 1) * chunk]
            landed(piece, part_s.at[j, k], part_r.at[j, k], (g, z, q))
        emb_rows = emb_rows + there[...]
    norm = row_norm(emb_rows)
    unit = emb_rows / norm
    unit_ref[...] = unit
    norm_ref[...] = jnp.broadcast_to(norm, norm_ref.shape)
    img[slot(p, own), :] = unit.astype(BF16)
    gather_start(img, img_s, img_r)

    line_land(1, text_at, txt_s, txt_r)
    line_send(2, text_at, txt_s, txt_r)
    line_send(0, hid_at, hid_s, hid_r)
    gather_finish(img, img_s, img_r)
    for step in range(2, blocks - 1):
        line_land(step, text_at, txt_s, txt_r)
        line_send(step + 1, text_at, txt_s, txt_r)
    hid_land(0)
    line_send(1, hid_at, hid_s, hid_r)

    count = blocks * texts
    sims = lax.dot_general(
        txt[...], img[...], (((1,), (1,)), ((), ())), preferred_element_type=F32
    )
    scale = jnp.exp(temp_ref[...])
    logits = scale * sims + bias_ref[...]
    at = lax.broadcasted_iota(jnp.int32, (count, 1), 0)
    column = at + (g * blocks * splits + x) * texts
    for j in range(1, blocks):
        column = column + jnp.where(at >= j * texts, (splits - 1) * texts, 0)
    match = column == pos_ref[...]
    signed = jnp.where(match, logits, -logits)
    small = jnp.exp(-jnp.abs(signed))
    loss_at = jnp.log1p(small) - jnp.minimum(signed, 0.0)
    slope = jnp.where(signed >= 0.0, small, 1.0) / (1.0 + small)
    slope = jnp.where(match, -slope, slope)
    wts[...] = (scale * slope).astype(BF16)

    for j in range(emb // chunk):
        c = slice(j * chunk, (j + 1) * chunk)
        gi_own[:, c] = lax.dot_general(
            wts[...], txt[:, c], (((0,), (0,)), ((), ())), preferred_element_type=F32
        )
    if pair == 2:
        for o in range(outer):
            send(gi_own.at[slot(o * pair + 1 - half, band), :], gi_pair.at[o],
                 gp_s.at[o], gp_r.at[o], sibling)

    for j in range(emb // chunk):
        c = slice(j * chunk, (j + 1) * chunk)
        value = jnp.dot(wts[...], img[:, c], preferred_element_type=F32)
        gt_send[:, c] = value.astype(BF16)
        gt_own[:, c] = value
    for k in range(1, blocks):
        q, device = along(k)
        send(gt_send.at[slot(q, texts), :], gt_recv.at[slot(z, texts), :],
             gt_s.at[k], gt_r.at[k], device)

    hid_land(1)
    line_send(2, hid_at, hid_s, hid_r)
    for o in range(outer):
        value = gi_own[slot(o * pair + half, band), :]
        if pair == 2:
            landed(gi_pair.at[o], gp_s.at[o], gp_r.at[o], sibling)
            value = value + gi_pair[o]
            gi_pair[o] = value
        gi_send[slot(o, band), :] = value.astype(BF16)
    for k in range(1, chips):
        c = to_chip(k)
        send(gi_send.at[slot(c, own), :], gi_recv.at[slot(chip, own), :],
             gi_s.at[k], gi_r.at[k], chip_device(c))

    def add_all(v):
        return jnp.sum(jnp.sum(v, axis=1, keepdims=True), axis=0, keepdims=True)

    line = lax.broadcasted_iota(jnp.int32, (8, LANES), 0)
    stat = jnp.where(line == 0, add_all(loss_at), 0.0)
    stat = jnp.where(line == 1, add_all(slope * sims), stat)
    stat = jnp.where(line == 2, add_all(slope), stat)
    stat_plane[p] = stat
    for k in range(1, plane):
        here = stat_plane.at[p]
        send(here, here, sp_s.at[k], sp_r.at[k], in_plane(k)[1])

    if pair == 2:
        grads = gi_pair[out, slot(x, own), :]
    else:
        grads = gi_own[slot(p, own), :]
    for k in range(1, chips):
        there = gi_recv.at[slot(from_chip(k), own), :]
        landed(there, gi_s.at[k], gi_r.at[k], chip_device(from_chip(k)))
        grads = grads + there[...].astype(F32)
    rounded = unit_backward(grads, unit_ref[...], norm_ref[:, :1]).astype(BF16)
    low[slot(p, own), :] = rounded
    for j in range(blocks):
        for i in range(groups):
            at = i * group_cols + j * cols
            col_send[j, :, i * width:i * width + cols] = rounded[:, at:at + cols]
    for k in range(1, blocks):
        q, device = along(k)
        send(col_send.at[q], col_mid.at[z], cz_s.at[k], cz_r.at[k], device)
    gather_start(low, low_s, low_r)
    col_mid[z] = col_send[z]

    for k in range(1, plane):
        there = stat_plane.at[from_plane(k)]
        landed(there, sp_s.at[k], sp_r.at[k], in_plane(k)[1])
    stat = stat_plane[0]
    for j in range(1, plane):
        stat = stat + stat_plane[j]
    stat_all[z] = stat
    for k in range(1, blocks):
        here = stat_all.at[z]
        send(here, here, sa_s.at[k], sa_r.at[k], along(k)[1])

    for k in range(1, blocks):
        landed(col_mid.at[from_along(k)], cz_s.at[k], cz_r.at[k], along(k)[1])
    for k in range(1, plane):
        q, device = in_plane(k)
        send(col_mid.at[:, :, slot(lax.div(q, splits), width)],
             col_all.at[:, slot(p, own), :], cp_s.at[k], cp_r.at[k], device)
    col_all[:, slot(p, own), :] = col_mid[:, :, slot(g, width)]
    gather_finish(low, low_s, low_r)
    for step in range(2, blocks - 1):
        hid_land(step)
        line_send(step + 1, hid_at, hid_s, hid_r)
    gimg_ref[...] = low[...]

    grads = gt_own[slot(z, texts), :]
    for k in range(1, blocks):
        there = gt_recv.at[slot(from_along(k), texts), :]
        landed(there, gt_s.at[k], gt_r.at[k], along(k)[1])
        grads = grads + there[...].astype(F32)
    text = txt_ref[...].astype(F32)
    norm = row_norm(text)
    gtxt_ref[...] = unit_backward(grads, text / norm, norm)

    for k in range(1, blocks):
        there = stat_all.at[from_along(k)]
        landed(there, sa_s.at[k], sa_r.at[k], along(k)[1])
    stat = stat_all[0]
    for j in range(1, blocks):
        stat = stat + stat_all[j]
    loss_ref[...] = stat[0:1, 0:1] / pairs
    gtemp_ref[...] = scale * stat[1:2, 0:1] / pairs
    gbias_ref[...] = stat[2:3, 0:1] / pairs

    if pair == 2:
        for k in range(1, blocks):
            q = from_along(k)
            there = hid_all.at[q, slot(1 - half, part_rows), :]
            landed(there, hp_s.at[q], hp_r.at[q], sibling)
            hid_pair(q).wait_send()
    for k in range(1, plane):
        there = col_all.at[:, slot(from_plane(k), own), :]
        landed(there, cp_s.at[k], cp_r.at[k], in_plane(k)[1])
    total[...] = jnp.zeros_like(total)
    for q in range(blocks):
        total[...] += lax.dot_general(
            col_all[q], hid_all[q], (((0,), (0,)), ((), ())), preferred_element_type=F32
        )
    gw_ref[...] = total[0:cols, :]
    line_sent(text_at, txt_s, txt_r)
    line_sent(hid_at, hid_s, hid_r)
    for c in sent:
        c.wait_send()


def on_device(image_hidden, image_weight, text_embed, positives, log_temp, bias):
    groups, blocks, splits = (lax.axis_size(a) for a in ("group", "blk", "mp"))
    plane = groups * splits
    rows, depth = image_hidden.shape
    emb = image_weight.shape[1]
    texts = text_embed.shape[0]
    own = rows // plane
    pair = 2 if groups % 2 == 0 else 1
    band = splits * own
    count = blocks * texts
    cols = emb // (groups * blocks)
    width = -(-cols // LANES) * LANES
    vmem = pl.BlockSpec(memory_space=pltpu.VMEM)
    dma = pltpu.SemaphoreType.DMA
    outs = pl.pallas_call(
        functools.partial(kernel, (groups, blocks, splits)),
        out_shape=[
            jax.ShapeDtypeStruct((1, 1), F32),
            jax.ShapeDtypeStruct((1, 1), F32),
            jax.ShapeDtypeStruct((1, 1), F32),
            jax.ShapeDtypeStruct((rows, emb), BF16),
            jax.ShapeDtypeStruct((texts, emb), F32),
            jax.ShapeDtypeStruct((cols, depth), F32),
        ],
        in_specs=[pl.BlockSpec(memory_space=pltpu.HBM)] * 4 + [vmem] * 2,
        out_specs=[vmem] * 6,
        scratch_shapes=[
            pltpu.VMEM((depth, rows), BF16),
            pltpu.VMEM((depth, emb), BF16),
            pltpu.VMEM((texts, emb), BF16),
            pltpu.VMEM((1, rows), jnp.int32),
            pltpu.VMEM((band, emb), F32),
            pltpu.VMEM((band, emb), F32),
            pltpu.VMEM((own, emb), F32),
            pltpu.VMEM((own, LANES), F32),
            pltpu.VMEM((rows, emb), BF16),
            pltpu.VMEM((count, emb), BF16),
            pltpu.VMEM((blocks, rows, depth), BF16),
            pltpu.VMEM((count, rows), BF16),
            pltpu.VMEM((rows, emb), F32),
            pltpu.VMEM((rows // pair // band, band, emb), F32),
            pltpu.VMEM((rows // pair, emb), BF16),
            pltpu.VMEM((rows // pair, emb), BF16),
            pltpu.VMEM((rows, emb), BF16),
            pltpu.VMEM((count, emb), BF16),
            pltpu.VMEM((count, emb), BF16),
            pltpu.VMEM((count, emb), F32),
            pltpu.VMEM((blocks, own, groups * width), BF16),
            pltpu.VMEM((blocks, own, groups * width), BF16),
            pltpu.VMEM((blocks, rows, width), BF16),
            pltpu.VMEM((plane, 8, LANES), F32),
            pltpu.VMEM((blocks, 8, LANES), F32),
            pltpu.VMEM((width, depth), F32),
            dma((3 + groups,)),
            dma((groups, splits)), dma((groups, splits)),
            dma((plane,)), dma((plane,)),
            dma((2 * blocks,)), dma((2 * blocks,)),
            dma((2 * blocks,)), dma((2 * blocks,)),
            dma((blocks,)), dma((blocks,)),
            dma((groups,)), dma((groups,)),
            dma((plane,)), dma((plane,)),
            dma((plane,)), dma((plane,)),
            dma((blocks,)), dma((blocks,)),
            dma((blocks,)), dma((blocks,)),
            dma((plane,)), dma((plane,)),
            dma((plane,)), dma((plane,)),
            dma((blocks,)), dma((blocks,)),
        ],
        compiler_params=pltpu.CompilerParams(
            collective_id=0, has_side_effects=True, vmem_limit_bytes=64 * 1024 * 1024 - 64 * 1024
        ),
        name="contrast",
    )(
        image_hidden.T, image_weight, text_embed, positives.reshape(1, rows),
        log_temp.reshape(1, 1), bias.reshape(1, 1),
    )
    loss, grad_temp, grad_bias, grad_image, grad_text, grad_weight = outs
    return (
        loss.reshape(1), grad_temp.reshape(1), grad_bias.reshape(1),
        grad_image.astype(F32), grad_text, grad_weight.T,
    )


def solution(mesh):
    in_specs = (P("blk", "mp"), P("mp", None), P(("group", "blk", "mp"), None), P("blk"), P(), P())
    out_specs = (
        P(),
        P(),
        P(),
        P("blk", None),
        P(("group", "blk", "mp"), None),
        P("mp", ("group", "blk")),
    )
    return jax.shard_map(
        on_device, mesh=mesh, in_specs=in_specs, out_specs=out_specs, check_vma=False
    )
```

```python
import functools

import jax
import jax.numpy as jnp
from jax import lax
from jax.experimental import pallas as pl
from jax.experimental.pallas import tpu as pltpu
from jax.sharding import PartitionSpec as P

MESH = pl.DeviceIdType.MESH
LANES = 128
LIMIT = 64 * 1024 * 1024 - 64 * 1024
F32 = jnp.float32
BF16 = jnp.bfloat16


def row_norm(values):
    return jnp.sqrt(jnp.sum(values * values, axis=1, keepdims=True) + 1e-06)


def unit_backward(grads, unit, norm_rows):
    return (grads - unit * jnp.sum(unit * grads, axis=1, keepdims=True)) / norm_rows


def kernel(
    sizes,
    hid_hbm, w_hbm, txt_hbm, pos_hbm, temp_ref, bias_ref,
    stat_ref, gimg_hbm, gtxt_hbm, gw_hbm,
    hid_ref, w_ref, txt_ref, pos_ref, part_recv, own_part, unit_ref, norm_ref, img, txt, hid_all,
    wts, gi_own, gi_pair, gi_send, gi_recv, low, gt_send, gt_recv, gt_own,
    col_send, col_mid, col_all, stat_plane, stat_all, total,
    gtxt_ref, gw_ref, load_s, store_s, part_s, part_r, img_s, img_r, txt_s, txt_r, hid_s, hid_r, hp_s, hp_r, gp_s, gp_r, gi_s, gi_r,
    low_s, low_r, gt_s, gt_r, cz_s, cz_r, cp_s, cp_r, sp_s, sp_r, sa_s, sa_r,
):
    groups, blocks, splits = sizes
    plane = groups * splits
    pair = 2 if groups % 2 == 0 else 1
    outer = groups // pair
    chips = outer * splits
    rows, emb = img.shape
    own = rows // plane
    band = splits * own
    texts = txt_ref.shape[0]
    pairs = rows * blocks
    group_cols = emb // groups
    cols = group_cols // blocks
    width = total.shape[0]
    part_rows = rows // pair
    chunk = group_cols
    g, z, x = lax.axis_index("group"), lax.axis_index("blk"), lax.axis_index("mp")
    p = g * splits + x
    half, out = lax.rem(g, pair), lax.div(g, pair)
    chip = out * splits + x
    sibling = (out * pair + (pair - 1 - half), z, x)

    def in_plane(k):
        q = lax.rem(p + k, plane)
        return q, (lax.div(q, splits), z, lax.rem(q, splits))

    def from_plane(k):
        return lax.rem(p + plane - k, plane)

    def on_chip(c, h):
        return (lax.div(c, splits) * pair + h) * splits + lax.rem(c, splits)

    def chip_device(c):
        return (lax.div(c, splits) * pair + half, z, lax.rem(c, splits))

    def to_chip(k):
        return lax.rem(chip + k, chips)

    def from_chip(k):
        return lax.rem(chip + chips - k, chips)

    def along(k):
        q = lax.rem(z + k, blocks)
        return q, (g, q, x)

    def from_along(k):
        return lax.rem(z + blocks - k, blocks)

    def slot(i, size):
        return pl.ds(pl.multiple_of(i * size, size), size)

    def copy(src, dst, send_sem, recv_sem, device):
        return pltpu.make_async_remote_copy(
            src_ref=src, dst_ref=dst, send_sem=send_sem, recv_sem=recv_sem,
            device_id=device, device_id_type=MESH,
        )

    sent = []

    def send(*args):
        c = copy(*args)
        c.start()
        sent.append(c)

    def landed(dst, send_sem, recv_sem, device):
        copy(dst, dst, send_sem, recv_sem, device).wait_recv()

    def gather_start(buf, s_sem, r_sem):
        here = buf.at[slot(p, own), :]
        for k in range(1, chips):
            send(here, here, s_sem.at[k], r_sem.at[k], chip_device(to_chip(k)))
        if pair == 2:
            send(here, here, s_sem.at[chips], r_sem.at[chips], sibling)

    def gather_finish(buf, s_sem, r_sem):
        for k in range(1, chips):
            there = buf.at[slot(on_chip(from_chip(k), half), own), :]
            landed(there, s_sem.at[k], r_sem.at[k], chip_device(from_chip(k)))
            if pair == 2:
                send(there, there, s_sem.at[chips + k], r_sem.at[chips + k], sibling)
        if pair == 2:
            for k in range(chips):
                there = buf.at[slot(on_chip(from_chip(k), 1 - half), own), :]
                landed(there, s_sem.at[chips + k], r_sem.at[chips + k], sibling)

    def line_copies(step, at, s_sem, r_sem):
        up = copy(at(z - step), at(z - step), s_sem.at[step], r_sem.at[step], (g, z + 1, x))
        down = copy(at(z + step), at(z + step), s_sem.at[blocks + step],
                    r_sem.at[blocks + step], (g, z - 1, x))
        return (((z - step >= 0) & (z + 1 < blocks), up),
                ((z + step < blocks) & (z - 1 >= 0), down))

    def line_send(step, at, s_sem, r_sem):
        if step < blocks - 1:
            for held, c in line_copies(step, at, s_sem, r_sem):
                pl.when(held)(c.start)

    def line_sent(at, s_sem, r_sem):
        for step in range(blocks - 1):
            for held, c in line_copies(step, at, s_sem, r_sem):
                pl.when(held)(c.wait_send)

    def line_land(step, at, s_sem, r_sem, then=None):
        if step >= blocks - 1:
            return
        for came, q, i, device in (
            (z - 1 - step >= 0, z - 1 - step, step, (g, z - 1, x)),
            (z + 1 + step < blocks, z + 1 + step, blocks + step, (g, z + 1, x)),
        ):
            @pl.when(came)
            def _():
                landed(at(q), s_sem.at[i], r_sem.at[i], device)
                if then is not None:
                    then(q)

    def text_at(q):
        return txt.at[slot(q, texts), :]

    def hid_at(q):
        return hid_all.at[q, slot(half, part_rows), :]

    def hid_pair(q):
        return copy(hid_at(q), hid_at(q), hp_s.at[q], hp_r.at[q], sibling)

    def hid_land(step):
        line_land(step, hid_at, hid_s, hid_r,
                  (lambda q: hid_pair(q).start()) if pair == 2 else None)

    loads = [
        pltpu.make_async_copy(hid_hbm, hid_ref, load_s.at[0]),
        pltpu.make_async_copy(txt_hbm, txt_ref, load_s.at[1]),
        pltpu.make_async_copy(pos_hbm, pos_ref, load_s.at[2]),
    ]
    for j in range(emb // chunk):
        at = slice(j * chunk, (j + 1) * chunk)
        loads.append(pltpu.make_async_copy(w_hbm.at[:, at], w_ref.at[:, at], load_s.at[3 + j]))
    for c in loads:
        c.start()

    barrier = pltpu.get_barrier_semaphore()
    for k in range(1, plane):
        pl.semaphore_signal(barrier, inc=1, device_id=in_plane(k)[1], device_id_type=MESH)
    for k in range(1, blocks):
        pl.semaphore_signal(barrier, inc=1, device_id=along(k)[1], device_id_type=MESH)

    loads[0].wait()
    hid_all[z] = hid_ref[...].T
    loads[1].wait()
    text = txt_ref[...].astype(F32)
    txt[slot(z, texts), :] = (text / row_norm(text)).astype(BF16)
    pl.semaphore_wait(barrier, plane - 1 + blocks - 1)
    line_send(0, text_at, txt_s, txt_r)
    mine = hid_all[z, slot(g, band), :]
    for j in range(emb // chunk):
        at = slice(j * chunk, (j + 1) * chunk)
        loads[3 + j].wait()
        own_part[:, at] = jnp.dot(mine, w_ref[:, at], preferred_element_type=F32)
        for k in range(1, splits):
            q = lax.rem(x + k, splits)
            send(own_part.at[slot(q, own), at], part_recv.at[slot(x, own), at],
                 part_s.at[j, k], part_r.at[j, k], (g, z, q))
    loads[2].wait()
    line_land(0, text_at, txt_s, txt_r)
    line_send(1, text_at, txt_s, txt_r)
    line_send(0, hid_at, hid_s, hid_r)

    emb_rows = own_part[slot(x, own), :]
    for k in range(1, splits):
        q = lax.rem(x + splits - k, splits)
        there = part_recv.at[slot(q, own), :]
        for j in range(emb // chunk):
            piece = part_recv.at[slot(q, own), j * chunk:(j + 1) * chunk]
            landed(piece, part_s.at[j, k], part_r.at[j, k], (g, z, q))
        emb_rows = emb_rows + there[...]
    norm = row_norm(emb_rows)
    unit = emb_rows / norm
    unit_ref[...] = unit
    norm_ref[...] = jnp.broadcast_to(norm, norm_ref.shape)
    img[slot(p, own), :] = unit.astype(BF16)
    gather_start(img, img_s, img_r)

    line_land(1, text_at, txt_s, txt_r)
    line_send(2, text_at, txt_s, txt_r)
    gather_finish(img, img_s, img_r)
    for step in range(2, blocks - 1):
        line_land(step, text_at, txt_s, txt_r)
        line_send(step + 1, text_at, txt_s, txt_r)

    count = blocks * texts
    sims = lax.dot_general(
        txt[...], img[...], (((1,), (1,)), ((), ())), preferred_element_type=F32
    )
    scale = jnp.exp(temp_ref[...])
    logits = scale * sims + bias_ref[...]
    at = lax.broadcasted_iota(jnp.int32, (count, 1), 0)
    column = at + (g * blocks * splits + x) * texts
    for j in range(1, blocks):
        column = column + jnp.where(at >= j * texts, (splits - 1) * texts, 0)
    match = column == pos_ref[...]
    signed = jnp.where(match, logits, -logits)
    small = jnp.exp(-jnp.abs(signed))
    loss_at = jnp.log1p(small) - jnp.minimum(signed, 0.0)
    slope = jnp.where(signed >= 0.0, small, 1.0) / (1.0 + small)
    slope = jnp.where(match, -slope, slope)
    wts[...] = (scale * slope).astype(BF16)

    for j in range(emb // chunk):
        c = slice(j * chunk, (j + 1) * chunk)
        gi_own[:, c] = lax.dot_general(
            wts[...], txt[:, c], (((0,), (0,)), ((), ())), preferred_element_type=F32
        )
    if pair == 2:
        for o in range(outer):
            send(gi_own.at[slot(o * pair + 1 - half, band), :], gi_pair.at[o],
                 gp_s.at[o], gp_r.at[o], sibling)

    hid_land(0)
    line_send(1, hid_at, hid_s, hid_r)
    for j in range(emb // chunk):
        c = slice(j * chunk, (j + 1) * chunk)
        value = jnp.dot(wts[...], img[:, c], preferred_element_type=F32)
        gt_send[:, c] = value.astype(BF16)
        gt_own[:, c] = value
    for k in range(1, blocks):
        q, device = along(k)
        send(gt_send.at[slot(q, texts), :], gt_recv.at[slot(z, texts), :],
             gt_s.at[k], gt_r.at[k], device)

    for o in range(outer):
        value = gi_own[slot(o * pair + half, band), :]
        if pair == 2:
            landed(gi_pair.at[o], gp_s.at[o], gp_r.at[o], sibling)
            value = value + gi_pair[o]
            gi_pair[o] = value
        gi_send[slot(o, band), :] = value.astype(BF16)
    for k in range(1, chips):
        c = to_chip(k)
        send(gi_send.at[slot(c, own), :], gi_recv.at[slot(chip, own), :],
             gi_s.at[k], gi_r.at[k], chip_device(c))

    def add_all(v):
        return jnp.sum(jnp.sum(v, axis=1, keepdims=True), axis=0, keepdims=True)

    line = lax.broadcasted_iota(jnp.int32, (8, LANES), 0)
    stat = jnp.where(line == 0, add_all(loss_at), 0.0)
    stat = jnp.where(line == 1, add_all(slope * sims), stat)
    stat = jnp.where(line == 2, add_all(slope), stat)
    stat_plane[p] = stat
    for k in range(1, plane):
        here = stat_plane.at[p]
        send(here, here, sp_s.at[k], sp_r.at[k], in_plane(k)[1])

    hid_land(1)
    line_send(2, hid_at, hid_s, hid_r)
    if pair == 2:
        grads = gi_pair[out, slot(x, own), :]
    else:
        grads = gi_own[slot(p, own), :]
    for k in range(1, chips):
        there = gi_recv.at[slot(from_chip(k), own), :]
        landed(there, gi_s.at[k], gi_r.at[k], chip_device(from_chip(k)))
        grads = grads + there[...].astype(F32)
    rounded = unit_backward(grads, unit_ref[...], norm_ref[:, :1]).astype(BF16)
    low[slot(p, own), :] = rounded
    for j in range(blocks):
        for i in range(groups):
            at = i * group_cols + j * cols
            col_send[j, :, i * width:i * width + cols] = rounded[:, at:at + cols]
    for k in range(1, blocks):
        q, device = along(k)
        send(col_send.at[q], col_mid.at[z], cz_s.at[k], cz_r.at[k], device)
    gather_start(low, low_s, low_r)
    col_mid[z] = col_send[z]

    for k in range(1, plane):
        there = stat_plane.at[from_plane(k)]
        landed(there, sp_s.at[k], sp_r.at[k], in_plane(k)[1])
    stat = stat_plane[0]
    for j in range(1, plane):
        stat = stat + stat_plane[j]
    stat_all[z] = stat
    for k in range(1, blocks):
        here = stat_all.at[z]
        send(here, here, sa_s.at[k], sa_r.at[k], along(k)[1])

    for k in range(1, blocks):
        landed(col_mid.at[from_along(k)], cz_s.at[k], cz_r.at[k], along(k)[1])
    for k in range(1, plane):
        q, device = in_plane(k)
        send(col_mid.at[:, :, slot(lax.div(q, splits), width)],
             col_all.at[:, slot(p, own), :], cp_s.at[k], cp_r.at[k], device)
    col_all[:, slot(p, own), :] = col_mid[:, :, slot(g, width)]
    gather_finish(low, low_s, low_r)
    for step in range(2, blocks - 1):
        hid_land(step)
        line_send(step + 1, hid_at, hid_s, hid_r)
    stores = [pltpu.make_async_copy(low, gimg_hbm, store_s.at[0])]
    stores[0].start()

    grads = gt_own[slot(z, texts), :]
    for k in range(1, blocks):
        there = gt_recv.at[slot(from_along(k), texts), :]
        landed(there, gt_s.at[k], gt_r.at[k], along(k)[1])
        grads = grads + there[...].astype(F32)
    text = txt_ref[...].astype(F32)
    norm = row_norm(text)
    gtxt_ref[...] = unit_backward(grads, text / norm, norm)
    stores.append(pltpu.make_async_copy(gtxt_ref, gtxt_hbm, store_s.at[1]))
    stores[1].start()

    for k in range(1, blocks):
        there = stat_all.at[from_along(k)]
        landed(there, sa_s.at[k], sa_r.at[k], along(k)[1])
    stat = stat_all[0]
    for j in range(1, blocks):
        stat = stat + stat_all[j]
    stat_ref[...] = jnp.where(line == 1, scale * stat, stat) / pairs

    if pair == 2:
        for k in range(1, blocks):
            q = from_along(k)
            there = hid_all.at[q, slot(1 - half, part_rows), :]
            landed(there, hp_s.at[q], hp_r.at[q], sibling)
            hid_pair(q).wait_send()
    for k in range(1, plane):
        there = col_all.at[:, slot(from_plane(k), own), :]
        landed(there, cp_s.at[k], cp_r.at[k], in_plane(k)[1])
    total[...] = jnp.zeros_like(total)
    for q in range(blocks):
        total[...] += lax.dot_general(
            col_all[q], hid_all[q], (((0,), (0,)), ((), ())), preferred_element_type=F32
        )
    gw_ref[...] = total[0:cols, :]
    stores.append(pltpu.make_async_copy(gw_ref, gw_hbm, store_s.at[2]))
    stores[2].start()
    line_sent(text_at, txt_s, txt_r)
    line_sent(hid_at, hid_s, hid_r)
    for c in sent:
        c.wait_send()
    for c in stores:
        c.wait()


def finish(parts, stat_ref, low_hbm, txt_hbm, w_hbm, loss_ref, gtemp_ref, gbias_ref,
           gimg_hbm, gtxt_hbm, gw_hbm, low, wide, sem_in, sem_out):
    whole = [
        pltpu.make_async_copy(txt_hbm, gtxt_hbm, sem_in.at[parts]),
        pltpu.make_async_copy(w_hbm, gw_hbm, sem_in.at[parts + 1]),
    ]
    size = low.shape[0] // parts
    cuts = [slice(j * size, (j + 1) * size) for j in range(parts)]
    loads = [
        pltpu.make_async_copy(low_hbm.at[c, :], low.at[c, :], sem_in.at[j])
        for j, c in enumerate(cuts)
    ]
    for c in loads + whole:
        c.start()
    loss_ref[...] = stat_ref[0:1, 0:1]
    gtemp_ref[...] = stat_ref[1:2, 0:1]
    gbias_ref[...] = stat_ref[2:3, 0:1]
    for j, c in enumerate(cuts):
        loads[j].wait()
        wide[c, :] = low[c, :].astype(F32)
        done = pltpu.make_async_copy(wide.at[c, :], gimg_hbm.at[c, :], sem_out.at[j])
        done.start()
        whole.append(done)
    for c in whole:
        c.wait()


def on_device(image_hidden, image_weight, text_embed, positives, log_temp, bias):
    groups, blocks, splits = (lax.axis_size(a) for a in ("group", "blk", "mp"))
    plane = groups * splits
    rows, depth = image_hidden.shape
    emb = image_weight.shape[1]
    texts = text_embed.shape[0]
    own = rows // plane
    pair = 2 if groups % 2 == 0 else 1
    band = splits * own
    count = blocks * texts
    cols = emb // (groups * blocks)
    width = -(-cols // LANES) * LANES
    vmem = pl.BlockSpec(memory_space=pltpu.VMEM)
    anywhere = pl.BlockSpec(memory_space=pl.ANY)
    dma = pltpu.SemaphoreType.DMA
    outs = pl.pallas_call(
        functools.partial(kernel, (groups, blocks, splits)),
        out_shape=[
            jax.ShapeDtypeStruct((8, LANES), F32),
            jax.ShapeDtypeStruct((rows, emb), BF16),
            jax.ShapeDtypeStruct((texts, emb), F32),
            jax.ShapeDtypeStruct((cols, depth), F32),
        ],
        in_specs=[anywhere] * 4 + [vmem] * 2,
        out_specs=[vmem] + [anywhere] * 3,
        scratch_shapes=[
            pltpu.VMEM((depth, rows), BF16),
            pltpu.VMEM((depth, emb), BF16),
            pltpu.VMEM((texts, emb), BF16),
            pltpu.VMEM((1, rows), jnp.int32),
            pltpu.VMEM((band, emb), F32),
            pltpu.VMEM((band, emb), F32),
            pltpu.VMEM((own, emb), F32),
            pltpu.VMEM((own, LANES), F32),
            pltpu.VMEM((rows, emb), BF16),
            pltpu.VMEM((count, emb), BF16),
            pltpu.VMEM((blocks, rows, depth), BF16),
            pltpu.VMEM((count, rows), BF16),
            pltpu.VMEM((rows, emb), F32),
            pltpu.VMEM((rows // pair // band, band, emb), F32),
            pltpu.VMEM((rows // pair, emb), BF16),
            pltpu.VMEM((rows // pair, emb), BF16),
            pltpu.VMEM((rows, emb), BF16),
            pltpu.VMEM((count, emb), BF16),
            pltpu.VMEM((count, emb), BF16),
            pltpu.VMEM((count, emb), F32),
            pltpu.VMEM((blocks, own, groups * width), BF16),
            pltpu.VMEM((blocks, own, groups * width), BF16),
            pltpu.VMEM((blocks, rows, width), BF16),
            pltpu.VMEM((plane, 8, LANES), F32),
            pltpu.VMEM((blocks, 8, LANES), F32),
            pltpu.VMEM((width, depth), F32),
            pltpu.VMEM((texts, emb), F32),
            pltpu.VMEM((cols, depth), F32),
            dma((3 + groups,)),
            dma((3,)),
            dma((groups, splits)), dma((groups, splits)),
            dma((plane,)), dma((plane,)),
            dma((2 * blocks,)), dma((2 * blocks,)),
            dma((2 * blocks,)), dma((2 * blocks,)),
            dma((blocks,)), dma((blocks,)),
            dma((groups,)), dma((groups,)),
            dma((plane,)), dma((plane,)),
            dma((plane,)), dma((plane,)),
            dma((blocks,)), dma((blocks,)),
            dma((blocks,)), dma((blocks,)),
            dma((plane,)), dma((plane,)),
            dma((plane,)), dma((plane,)),
            dma((blocks,)), dma((blocks,)),
        ],
        compiler_params=pltpu.CompilerParams(
            collective_id=0, has_side_effects=True, vmem_limit_bytes=LIMIT
        ),
        name="contrast",
    )(
        image_hidden.T, image_weight, text_embed, positives.reshape(1, rows),
        log_temp.reshape(1, 1), bias.reshape(1, 1),
    )
    parts = 4 if rows % 64 == 0 else 1
    loss, grad_temp, grad_bias, grad_image, grad_text, grad_weight = pl.pallas_call(
        functools.partial(finish, parts),
        out_shape=[
            jax.ShapeDtypeStruct((1, 1), F32),
            jax.ShapeDtypeStruct((1, 1), F32),
            jax.ShapeDtypeStruct((1, 1), F32),
            jax.ShapeDtypeStruct((rows, emb), F32),
            jax.ShapeDtypeStruct((texts, emb), F32),
            jax.ShapeDtypeStruct((cols, depth), F32),
        ],
        in_specs=[vmem] + [anywhere] * 3,
        out_specs=[vmem] * 3 + [anywhere] * 3,
        scratch_shapes=[
            pltpu.VMEM((rows, emb), BF16),
            pltpu.VMEM((rows, emb), F32),
            dma((parts + 2,)),
            dma((parts,)),
        ],
        compiler_params=pltpu.CompilerParams(vmem_limit_bytes=LIMIT),
        name="finish",
    )(*outs)
    return (
        loss.reshape(1), grad_temp.reshape(1), grad_bias.reshape(1),
        grad_image, grad_text, grad_weight.T,
    )


def solution(mesh):
    in_specs = (P("blk", "mp"), P("mp", None), P(("group", "blk", "mp"), None), P("blk"), P(), P())
    out_specs = (
        P(),
        P(),
        P(),
        P("blk", None),
        P(("group", "blk", "mp"), None),
        P("mp", ("group", "blk")),
    )
    return jax.shard_map(
        on_device, mesh=mesh, in_specs=in_specs, out_specs=out_specs, check_vma=False
    )
```

```python
import functools

import jax
import jax.numpy as jnp
from jax import lax
from jax.experimental import pallas as pl
from jax.experimental.pallas import tpu as pltpu
from jax.sharding import PartitionSpec as P

MESH = pl.DeviceIdType.MESH
LANES = 128
LIMIT = 64 * 1024 * 1024 - 64 * 1024
F32 = jnp.float32
BF16 = jnp.bfloat16


def row_norm(values):
    return jnp.sqrt(jnp.sum(values * values, axis=1, keepdims=True) + 1e-06)


def unit_backward(grads, unit, norm_rows):
    return (grads - unit * jnp.sum(unit * grads, axis=1, keepdims=True)) / norm_rows


def kernel(
    sizes,
    hid_hbm, w_hbm, txt_hbm, pos_hbm, temp_ref, bias_ref,
    stat_ref, gimg_hbm, gtxt_hbm, gw_hbm,
    hid_ref, w_ref, txt_ref, pos_ref, part_recv, own_part, unit_ref, norm_ref, img, txt, hid_all,
    wts, gi_own, gi_pair, gi_send, gi_recv, low, gt_send, gt_recv, gt_own,
    col_send, col_mid, col_all, stat_plane, stat_all, total,
    gtxt_ref, gw_ref, load_s, store_s, part_s, part_r, img_s, img_r, txt_s, txt_r, hid_s, hid_r, hp_s, hp_r, gp_s, gp_r, gi_s, gi_r,
    low_s, low_r, gt_s, gt_r, cz_s, cz_r, cp_s, cp_r, sp_s, sp_r, sa_s, sa_r,
):
    groups, blocks, splits = sizes
    plane = groups * splits
    pair = 2 if groups % 2 == 0 else 1
    outer = groups // pair
    chips = outer * splits
    rows, emb = img.shape
    own = rows // plane
    band = splits * own
    texts = txt_ref.shape[0]
    pairs = rows * blocks
    group_cols = emb // groups
    cols = group_cols // blocks
    width = total.shape[0]
    part_rows = rows // pair
    chunk = group_cols
    g, z, x = lax.axis_index("group"), lax.axis_index("blk"), lax.axis_index("mp")
    p = g * splits + x
    half, out = lax.rem(g, pair), lax.div(g, pair)
    chip = out * splits + x
    sibling = (out * pair + (pair - 1 - half), z, x)

    def in_plane(k):
        q = lax.rem(p + k, plane)
        return q, (lax.div(q, splits), z, lax.rem(q, splits))

    def from_plane(k):
        return lax.rem(p + plane - k, plane)

    def on_chip(c, h):
        return (lax.div(c, splits) * pair + h) * splits + lax.rem(c, splits)

    def chip_device(c):
        return (lax.div(c, splits) * pair + half, z, lax.rem(c, splits))

    def to_chip(k):
        return lax.rem(chip + k, chips)

    def from_chip(k):
        return lax.rem(chip + chips - k, chips)

    def along(k):
        q = lax.rem(z + k, blocks)
        return q, (g, q, x)

    def from_along(k):
        return lax.rem(z + blocks - k, blocks)

    def slot(i, size):
        return pl.ds(pl.multiple_of(i * size, size), size)

    def copy(src, dst, send_sem, recv_sem, device):
        return pltpu.make_async_remote_copy(
            src_ref=src, dst_ref=dst, send_sem=send_sem, recv_sem=recv_sem,
            device_id=device, device_id_type=MESH,
        )

    sent = []

    def send(*args):
        c = copy(*args)
        c.start()
        sent.append(c)

    def landed(dst, send_sem, recv_sem, device):
        copy(dst, dst, send_sem, recv_sem, device).wait_recv()

    def gather_start(buf, s_sem, r_sem):
        here = buf.at[slot(p, own), :]
        for k in range(1, chips):
            send(here, here, s_sem.at[k], r_sem.at[k], chip_device(to_chip(k)))
        if pair == 2:
            send(here, here, s_sem.at[chips], r_sem.at[chips], sibling)

    def gather_finish(buf, s_sem, r_sem):
        for k in range(1, chips):
            there = buf.at[slot(on_chip(from_chip(k), half), own), :]
            landed(there, s_sem.at[k], r_sem.at[k], chip_device(from_chip(k)))
            if pair == 2:
                send(there, there, s_sem.at[chips + k], r_sem.at[chips + k], sibling)
        if pair == 2:
            for k in range(chips):
                there = buf.at[slot(on_chip(from_chip(k), 1 - half), own), :]
                landed(there, s_sem.at[chips + k], r_sem.at[chips + k], sibling)

    def line_copies(step, at, s_sem, r_sem):
        up = copy(at(z - step), at(z - step), s_sem.at[step], r_sem.at[step], (g, z + 1, x))
        down = copy(at(z + step), at(z + step), s_sem.at[blocks + step],
                    r_sem.at[blocks + step], (g, z - 1, x))
        return (((z - step >= 0) & (z + 1 < blocks), up),
                ((z + step < blocks) & (z - 1 >= 0), down))

    def line_send(step, at, s_sem, r_sem):
        if step < blocks - 1:
            for held, c in line_copies(step, at, s_sem, r_sem):
                pl.when(held)(c.start)

    def line_sent(at, s_sem, r_sem):
        for step in range(blocks - 1):
            for held, c in line_copies(step, at, s_sem, r_sem):
                pl.when(held)(c.wait_send)

    def line_land(step, at, s_sem, r_sem, then=None):
        if step >= blocks - 1:
            return
        for came, q, i, device in (
            (z - 1 - step >= 0, z - 1 - step, step, (g, z - 1, x)),
            (z + 1 + step < blocks, z + 1 + step, blocks + step, (g, z + 1, x)),
        ):
            @pl.when(came)
            def _():
                landed(at(q), s_sem.at[i], r_sem.at[i], device)
                if then is not None:
                    then(q)

    def text_at(q):
        return txt.at[slot(q, texts), :]

    def hid_at(q):
        return hid_all.at[q, slot(half, part_rows), :]

    def hid_pair(q):
        return copy(hid_at(q), hid_at(q), hp_s.at[q], hp_r.at[q], sibling)

    def hid_land(step):
        line_land(step, hid_at, hid_s, hid_r,
                  (lambda q: hid_pair(q).start()) if pair == 2 else None)

    loads = [
        pltpu.make_async_copy(hid_hbm, hid_ref, load_s.at[0]),
        pltpu.make_async_copy(txt_hbm, txt_ref, load_s.at[1]),
        pltpu.make_async_copy(pos_hbm, pos_ref, load_s.at[2]),
    ]
    for j in range(emb // chunk):
        at = slice(j * chunk, (j + 1) * chunk)
        loads.append(pltpu.make_async_copy(w_hbm.at[:, at], w_ref.at[:, at], load_s.at[3 + j]))
    for c in loads:
        c.start()

    barrier = pltpu.get_barrier_semaphore()
    for k in range(1, plane):
        pl.semaphore_signal(barrier, inc=1, device_id=in_plane(k)[1], device_id_type=MESH)
    for k in range(1, blocks):
        pl.semaphore_signal(barrier, inc=1, device_id=along(k)[1], device_id_type=MESH)

    loads[0].wait()
    hid_all[z] = hid_ref[...].T
    loads[1].wait()
    text = txt_ref[...].astype(F32)
    txt[slot(z, texts), :] = (text / row_norm(text)).astype(BF16)
    pl.semaphore_wait(barrier, plane - 1 + blocks - 1)
    line_send(0, text_at, txt_s, txt_r)
    mine = hid_all[z, slot(g, band), :]
    for j in range(emb // chunk):
        at = slice(j * chunk, (j + 1) * chunk)
        loads[3 + j].wait()
        own_part[:, at] = jnp.dot(mine, w_ref[:, at], preferred_element_type=F32)
        for k in range(1, splits):
            q = lax.rem(x + k, splits)
            send(own_part.at[slot(q, own), at], part_recv.at[slot(x, own), at],
                 part_s.at[j, k], part_r.at[j, k], (g, z, q))
    loads[2].wait()
    line_land(0, text_at, txt_s, txt_r)
    line_send(1, text_at, txt_s, txt_r)
    line_send(0, hid_at, hid_s, hid_r)

    emb_rows = own_part[slot(x, own), :]
    for k in range(1, splits):
        q = lax.rem(x + splits - k, splits)
        there = part_recv.at[slot(q, own), :]
        for j in range(emb // chunk):
            piece = part_recv.at[slot(q, own), j * chunk:(j + 1) * chunk]
            landed(piece, part_s.at[j, k], part_r.at[j, k], (g, z, q))
        emb_rows = emb_rows + there[...]
    norm = row_norm(emb_rows)
    unit = emb_rows / norm
    unit_ref[...] = unit
    norm_ref[...] = jnp.broadcast_to(norm, norm_ref.shape)
    img[slot(p, own), :] = unit.astype(BF16)
    gather_start(img, img_s, img_r)

    line_land(1, text_at, txt_s, txt_r)
    line_send(2, text_at, txt_s, txt_r)
    gather_finish(img, img_s, img_r)
    for step in range(2, blocks - 1):
        line_land(step, text_at, txt_s, txt_r)
        line_send(step + 1, text_at, txt_s, txt_r)

    count = blocks * texts
    sims = lax.dot_general(
        txt[...], img[...], (((1,), (1,)), ((), ())), preferred_element_type=F32
    )
    scale = jnp.exp(temp_ref[...])
    logits = scale * sims + bias_ref[...]
    at = lax.broadcasted_iota(jnp.int32, (count, 1), 0)
    column = at + (g * blocks * splits + x) * texts
    for j in range(1, blocks):
        column = column + jnp.where(at >= j * texts, (splits - 1) * texts, 0)
    match = column == pos_ref[...]
    signed = jnp.where(match, logits, -logits)
    small = jnp.exp(-jnp.abs(signed))
    loss_at = jnp.log1p(small) - jnp.minimum(signed, 0.0)
    slope = jnp.where(signed >= 0.0, small, 1.0) / (1.0 + small)
    slope = jnp.where(match, -slope, slope)
    wts[...] = (scale * slope).astype(BF16)

    for j in range(emb // chunk):
        c = slice(j * chunk, (j + 1) * chunk)
        gi_own[:, c] = lax.dot_general(
            wts[...], txt[:, c], (((0,), (0,)), ((), ())), preferred_element_type=F32
        )
    if pair == 2:
        for o in range(outer):
            send(gi_own.at[slot(o * pair + 1 - half, band), :], gi_pair.at[o],
                 gp_s.at[o], gp_r.at[o], sibling)

    hid_land(0)
    line_send(1, hid_at, hid_s, hid_r)
    for j in range(emb // chunk):
        c = slice(j * chunk, (j + 1) * chunk)
        value = jnp.dot(wts[...], img[:, c], preferred_element_type=F32)
        gt_send[:, c] = value.astype(BF16)
        gt_own[:, c] = value
    for k in range(1, blocks):
        q, device = along(k)
        send(gt_send.at[slot(q, texts), :], gt_recv.at[slot(z, texts), :],
             gt_s.at[k], gt_r.at[k], device)

    for o in range(outer):
        value = gi_own[slot(o * pair + half, band), :]
        if pair == 2:
            landed(gi_pair.at[o], gp_s.at[o], gp_r.at[o], sibling)
            value = value + gi_pair[o]
            gi_pair[o] = value
        gi_send[slot(o, band), :] = value.astype(BF16)
    for k in range(1, chips):
        c = to_chip(k)
        send(gi_send.at[slot(c, own), :], gi_recv.at[slot(chip, own), :],
             gi_s.at[k], gi_r.at[k], chip_device(c))

    def add_all(v):
        return jnp.sum(jnp.sum(v, axis=1, keepdims=True), axis=0, keepdims=True)

    line = lax.broadcasted_iota(jnp.int32, (8, LANES), 0)
    stat = jnp.where(line == 0, add_all(loss_at), 0.0)
    stat = jnp.where(line == 1, add_all(slope * sims), stat)
    stat = jnp.where(line == 2, add_all(slope), stat)
    stat_plane[p] = stat
    for k in range(1, plane):
        here = stat_plane.at[p]
        send(here, here, sp_s.at[k], sp_r.at[k], in_plane(k)[1])

    hid_land(1)
    line_send(2, hid_at, hid_s, hid_r)
    if pair == 2:
        grads = gi_pair[out, slot(x, own), :]
    else:
        grads = gi_own[slot(p, own), :]
    for k in range(1, chips):
        there = gi_recv.at[slot(from_chip(k), own), :]
        landed(there, gi_s.at[k], gi_r.at[k], chip_device(from_chip(k)))
        grads = grads + there[...].astype(F32)
    rounded = unit_backward(grads, unit_ref[...], norm_ref[:, :1]).astype(BF16)
    low[slot(p, own), :] = rounded
    for j in range(blocks):
        for i in range(groups):
            at = i * group_cols + j * cols
            col_send[j, :, i * width:i * width + cols] = rounded[:, at:at + cols]
    for k in range(1, blocks):
        q, device = along(k)
        send(col_send.at[q], col_mid.at[z], cz_s.at[k], cz_r.at[k], device)
    gather_start(low, low_s, low_r)
    col_mid[z] = col_send[z]

    for k in range(1, plane):
        there = stat_plane.at[from_plane(k)]
        landed(there, sp_s.at[k], sp_r.at[k], in_plane(k)[1])
    stat = stat_plane[0]
    for j in range(1, plane):
        stat = stat + stat_plane[j]
    stat_all[z] = stat
    for k in range(1, blocks):
        here = stat_all.at[z]
        send(here, here, sa_s.at[k], sa_r.at[k], along(k)[1])

    for k in range(1, blocks):
        landed(col_mid.at[from_along(k)], cz_s.at[k], cz_r.at[k], along(k)[1])
    for k in range(1, plane):
        q, device = in_plane(k)
        send(col_mid.at[:, :, slot(lax.div(q, splits), width)],
             col_all.at[:, slot(p, own), :], cp_s.at[k], cp_r.at[k], device)
    col_all[:, slot(p, own), :] = col_mid[:, :, slot(g, width)]
    gather_finish(low, low_s, low_r)
    for step in range(2, blocks - 1):
        hid_land(step)
        line_send(step + 1, hid_at, hid_s, hid_r)
    stores = [pltpu.make_async_copy(low, gimg_hbm, store_s.at[0])]
    stores[0].start()

    grads = gt_own[slot(z, texts), :]
    for k in range(1, blocks):
        there = gt_recv.at[slot(from_along(k), texts), :]
        landed(there, gt_s.at[k], gt_r.at[k], along(k)[1])
        grads = grads + there[...].astype(F32)
    text = txt_ref[...].astype(F32)
    norm = row_norm(text)
    gtxt_ref[...] = unit_backward(grads, text / norm, norm)
    stores.append(pltpu.make_async_copy(gtxt_ref, gtxt_hbm, store_s.at[1]))
    stores[1].start()

    for k in range(1, blocks):
        there = stat_all.at[from_along(k)]
        landed(there, sa_s.at[k], sa_r.at[k], along(k)[1])
    stat = stat_all[0]
    for j in range(1, blocks):
        stat = stat + stat_all[j]
    stat_ref[...] = jnp.where(line == 1, scale * stat, stat) / pairs

    if pair == 2:
        for k in range(1, blocks):
            q = from_along(k)
            there = hid_all.at[q, slot(1 - half, part_rows), :]
            landed(there, hp_s.at[q], hp_r.at[q], sibling)
            hid_pair(q).wait_send()
    for k in range(1, plane):
        there = col_all.at[:, slot(from_plane(k), own), :]
        landed(there, cp_s.at[k], cp_r.at[k], in_plane(k)[1])
    total[...] = jnp.zeros_like(total)
    for q in range(blocks):
        total[...] += lax.dot_general(
            col_all[q], hid_all[q], (((0,), (0,)), ((), ())), preferred_element_type=F32
        )
    gw_ref[...] = total[0:cols, :]
    stores.append(pltpu.make_async_copy(gw_ref, gw_hbm, store_s.at[2]))
    stores[2].start()
    line_sent(text_at, txt_s, txt_r)
    line_sent(hid_at, hid_s, hid_r)
    for c in sent:
        c.wait_send()
    for c in stores:
        c.wait()


def finish(parts, stat_ref, low_hbm, txt_hbm, w_hbm, loss_ref, gtemp_ref, gbias_ref,
           gimg_hbm, gtxt_hbm, gw_hbm, low, wide, txt, wgt, sem_in, sem_out):
    size = low.shape[0] // parts
    cuts = [slice(j * size, (j + 1) * size) for j in range(parts)]
    loads = [
        pltpu.make_async_copy(low_hbm.at[c, :], low.at[c, :], sem_in.at[j])
        for j, c in enumerate(cuts)
    ]
    loads.append(pltpu.make_async_copy(txt_hbm, txt, sem_in.at[parts]))
    loads.append(pltpu.make_async_copy(w_hbm, wgt, sem_in.at[parts + 1]))
    for c in loads:
        c.start()
    stores = []
    loss_ref[...] = stat_ref[0:1, 0:1]
    gtemp_ref[...] = stat_ref[1:2, 0:1]
    gbias_ref[...] = stat_ref[2:3, 0:1]
    for j, c in enumerate(cuts):
        loads[j].wait()
        wide[c, :] = low[c, :].astype(F32)
        done = pltpu.make_async_copy(wide.at[c, :], gimg_hbm.at[c, :], sem_out.at[j])
        done.start()
        stores.append(done)
    for j, (buf, out) in enumerate(((txt, gtxt_hbm), (wgt, gw_hbm))):
        loads[parts + j].wait()
        done = pltpu.make_async_copy(buf, out, sem_out.at[parts + j])
        done.start()
        stores.append(done)
    for c in stores:
        c.wait()


def on_device(image_hidden, image_weight, text_embed, positives, log_temp, bias):
    groups, blocks, splits = (lax.axis_size(a) for a in ("group", "blk", "mp"))
    plane = groups * splits
    rows, depth = image_hidden.shape
    emb = image_weight.shape[1]
    texts = text_embed.shape[0]
    own = rows // plane
    pair = 2 if groups % 2 == 0 else 1
    band = splits * own
    count = blocks * texts
    cols = emb // (groups * blocks)
    width = -(-cols // LANES) * LANES
    vmem = pl.BlockSpec(memory_space=pltpu.VMEM)
    anywhere = pl.BlockSpec(memory_space=pl.ANY)
    dma = pltpu.SemaphoreType.DMA
    outs = pl.pallas_call(
        functools.partial(kernel, (groups, blocks, splits)),
        out_shape=[
            jax.ShapeDtypeStruct((8, LANES), F32),
            jax.ShapeDtypeStruct((rows, emb), BF16),
            jax.ShapeDtypeStruct((texts, emb), F32),
            jax.ShapeDtypeStruct((cols, depth), F32),
        ],
        in_specs=[anywhere] * 4 + [vmem] * 2,
        out_specs=[vmem] + [anywhere] * 3,
        scratch_shapes=[
            pltpu.VMEM((depth, rows), BF16),
            pltpu.VMEM((depth, emb), BF16),
            pltpu.VMEM((texts, emb), BF16),
            pltpu.VMEM((1, rows), jnp.int32),
            pltpu.VMEM((band, emb), F32),
            pltpu.VMEM((band, emb), F32),
            pltpu.VMEM((own, emb), F32),
            pltpu.VMEM((own, LANES), F32),
            pltpu.VMEM((rows, emb), BF16),
            pltpu.VMEM((count, emb), BF16),
            pltpu.VMEM((blocks, rows, depth), BF16),
            pltpu.VMEM((count, rows), BF16),
            pltpu.VMEM((rows, emb), F32),
            pltpu.VMEM((rows // pair // band, band, emb), F32),
            pltpu.VMEM((rows // pair, emb), BF16),
            pltpu.VMEM((rows // pair, emb), BF16),
            pltpu.VMEM((rows, emb), BF16),
            pltpu.VMEM((count, emb), BF16),
            pltpu.VMEM((count, emb), BF16),
            pltpu.VMEM((count, emb), F32),
            pltpu.VMEM((blocks, own, groups * width), BF16),
            pltpu.VMEM((blocks, own, groups * width), BF16),
            pltpu.VMEM((blocks, rows, width), BF16),
            pltpu.VMEM((plane, 8, LANES), F32),
            pltpu.VMEM((blocks, 8, LANES), F32),
            pltpu.VMEM((width, depth), F32),
            pltpu.VMEM((texts, emb), F32),
            pltpu.VMEM((cols, depth), F32),
            dma((3 + groups,)),
            dma((3,)),
            dma((groups, splits)), dma((groups, splits)),
            dma((plane,)), dma((plane,)),
            dma((2 * blocks,)), dma((2 * blocks,)),
            dma((2 * blocks,)), dma((2 * blocks,)),
            dma((blocks,)), dma((blocks,)),
            dma((groups,)), dma((groups,)),
            dma((plane,)), dma((plane,)),
            dma((plane,)), dma((plane,)),
            dma((blocks,)), dma((blocks,)),
            dma((blocks,)), dma((blocks,)),
            dma((plane,)), dma((plane,)),
            dma((plane,)), dma((plane,)),
            dma((blocks,)), dma((blocks,)),
        ],
        compiler_params=pltpu.CompilerParams(
            collective_id=0, has_side_effects=True, vmem_limit_bytes=LIMIT
        ),
        name="contrast",
    )(
        image_hidden.T, image_weight, text_embed, positives.reshape(1, rows),
        log_temp.reshape(1, 1), bias.reshape(1, 1),
    )
    parts = 4 if rows % 64 == 0 else 1
    loss, grad_temp, grad_bias, grad_image, grad_text, grad_weight = pl.pallas_call(
        functools.partial(finish, parts),
        out_shape=[
            jax.ShapeDtypeStruct((1, 1), F32),
            jax.ShapeDtypeStruct((1, 1), F32),
            jax.ShapeDtypeStruct((1, 1), F32),
            jax.ShapeDtypeStruct((rows, emb), F32),
            jax.ShapeDtypeStruct((texts, emb), F32),
            jax.ShapeDtypeStruct((cols, depth), F32),
        ],
        in_specs=[vmem] + [anywhere] * 3,
        out_specs=[vmem] * 3 + [anywhere] * 3,
        scratch_shapes=[
            pltpu.VMEM((rows, emb), BF16),
            pltpu.VMEM((rows, emb), F32),
            pltpu.VMEM((texts, emb), F32),
            pltpu.VMEM((cols, depth), F32),
            dma((parts + 2,)),
            dma((parts + 2,)),
        ],
        compiler_params=pltpu.CompilerParams(vmem_limit_bytes=LIMIT),
        name="finish",
    )(*outs)
    return (
        loss.reshape(1), grad_temp.reshape(1), grad_bias.reshape(1),
        grad_image, grad_text, grad_weight.T,
    )


def solution(mesh):
    in_specs = (P("blk", "mp"), P("mp", None), P(("group", "blk", "mp"), None), P("blk"), P(), P())
    out_specs = (
        P(),
        P(),
        P(),
        P("blk", None),
        P(("group", "blk", "mp"), None),
        P("mp", ("group", "blk")),
    )
    return jax.shard_map(
        on_device, mesh=mesh, in_specs=in_specs, out_specs=out_specs, check_vma=False
    )
```

```python
import functools

import jax
import jax.numpy as jnp
from jax import lax
from jax.experimental import pallas as pl
from jax.experimental.pallas import tpu as pltpu
from jax.sharding import PartitionSpec as P

MESH = pl.DeviceIdType.MESH
LANES = 128
LIMIT = 64 * 1024 * 1024 - 64 * 1024
F32 = jnp.float32
BF16 = jnp.bfloat16


def row_norm(values):
    return jnp.sqrt(jnp.sum(values * values, axis=1, keepdims=True) + 1e-06)


def unit_backward(grads, unit, norm_rows):
    return (grads - unit * jnp.sum(unit * grads, axis=1, keepdims=True)) / norm_rows


def kernel(
    sizes,
    hid_hbm, w_hbm, txt_hbm, pos_hbm, temp_ref, bias_ref,
    stat_ref, gimg_hbm, gtxt_hbm, gw_hbm,
    hid_ref, w_ref, txt_ref, pos_ref, part_recv, own_part, unit_ref, norm_ref, img, txt, hid_all,
    wts, gi_own, gi_pair, gi_send, gi_recv, low, gt_send, gt_recv, gt_own,
    col_send, col_mid, col_all, stat_plane, stat_all, total,
    gtxt_ref, gw_ref, load_s, store_s, part_s, part_r, img_s, img_r, txt_s, txt_r, hid_s, hid_r, hp_s, hp_r, gp_s, gp_r, gi_s, gi_r,
    low_s, low_r, gt_s, gt_r, cz_s, cz_r, cp_s, cp_r, sp_s, sp_r, sa_s, sa_r,
):
    groups, blocks, splits = sizes
    plane = groups * splits
    pair = 2 if groups % 2 == 0 else 1
    outer = groups // pair
    chips = outer * splits
    rows, emb = img.shape
    own = rows // plane
    band = splits * own
    texts = txt_ref.shape[0]
    pairs = rows * blocks
    group_cols = emb // groups
    cols = group_cols // blocks
    width = total.shape[0]
    part_rows = rows // pair
    chunk = group_cols
    g, z, x = lax.axis_index("group"), lax.axis_index("blk"), lax.axis_index("mp")
    p = g * splits + x
    half, out = lax.rem(g, pair), lax.div(g, pair)
    chip = out * splits + x
    sibling = (out * pair + (pair - 1 - half), z, x)

    def in_plane(k):
        q = lax.rem(p + k, plane)
        return q, (lax.div(q, splits), z, lax.rem(q, splits))

    def from_plane(k):
        return lax.rem(p + plane - k, plane)

    def on_chip(c, h):
        return (lax.div(c, splits) * pair + h) * splits + lax.rem(c, splits)

    def chip_device(c):
        return (lax.div(c, splits) * pair + half, z, lax.rem(c, splits))

    def to_chip(k):
        return lax.rem(chip + k, chips)

    def from_chip(k):
        return lax.rem(chip + chips - k, chips)

    def along(k):
        q = lax.rem(z + k, blocks)
        return q, (g, q, x)

    def from_along(k):
        return lax.rem(z + blocks - k, blocks)

    def slot(i, size):
        return pl.ds(pl.multiple_of(i * size, size), size)

    def copy(src, dst, send_sem, recv_sem, device):
        return pltpu.make_async_remote_copy(
            src_ref=src, dst_ref=dst, send_sem=send_sem, recv_sem=recv_sem,
            device_id=device, device_id_type=MESH,
        )

    sent = []

    def send(*args):
        c = copy(*args)
        c.start()
        sent.append(c)

    def landed(dst, send_sem, recv_sem, device):
        copy(dst, dst, send_sem, recv_sem, device).wait_recv()

    def gather_start(buf, s_sem, r_sem):
        here = buf.at[slot(p, own), :]
        for k in range(1, chips):
            send(here, here, s_sem.at[k], r_sem.at[k], chip_device(to_chip(k)))
        if pair == 2:
            send(here, here, s_sem.at[chips], r_sem.at[chips], sibling)

    def gather_finish(buf, s_sem, r_sem):
        for k in range(1, chips):
            there = buf.at[slot(on_chip(from_chip(k), half), own), :]
            landed(there, s_sem.at[k], r_sem.at[k], chip_device(from_chip(k)))
            if pair == 2:
                send(there, there, s_sem.at[chips + k], r_sem.at[chips + k], sibling)
        if pair == 2:
            for k in range(chips):
                there = buf.at[slot(on_chip(from_chip(k), 1 - half), own), :]
                landed(there, s_sem.at[chips + k], r_sem.at[chips + k], sibling)

    def line_copies(step, at, s_sem, r_sem):
        up = copy(at(z - step), at(z - step), s_sem.at[step], r_sem.at[step], (g, z + 1, x))
        down = copy(at(z + step), at(z + step), s_sem.at[blocks + step],
                    r_sem.at[blocks + step], (g, z - 1, x))
        return (((z - step >= 0) & (z + 1 < blocks), up),
                ((z + step < blocks) & (z - 1 >= 0), down))

    def line_send(step, at, s_sem, r_sem):
        if step < blocks - 1:
            for held, c in line_copies(step, at, s_sem, r_sem):
                pl.when(held)(c.start)

    def line_sent(at, s_sem, r_sem):
        for step in range(blocks - 1):
            for held, c in line_copies(step, at, s_sem, r_sem):
                pl.when(held)(c.wait_send)

    def line_land(step, at, s_sem, r_sem, then=None):
        if step >= blocks - 1:
            return
        for came, q, i, device in (
            (z - 1 - step >= 0, z - 1 - step, step, (g, z - 1, x)),
            (z + 1 + step < blocks, z + 1 + step, blocks + step, (g, z + 1, x)),
        ):
            @pl.when(came)
            def _():
                landed(at(q), s_sem.at[i], r_sem.at[i], device)
                if then is not None:
                    then(q)

    def text_at(q):
        return txt.at[slot(q, texts), :]

    def hid_at(q):
        return hid_all.at[q, slot(half, part_rows), :]

    def hid_pair(q):
        return copy(hid_at(q), hid_at(q), hp_s.at[q], hp_r.at[q], sibling)

    def hid_land(step):
        line_land(step, hid_at, hid_s, hid_r,
                  (lambda q: hid_pair(q).start()) if pair == 2 else None)

    loads = [
        pltpu.make_async_copy(hid_hbm, hid_ref, load_s.at[0]),
        pltpu.make_async_copy(txt_hbm, txt_ref, load_s.at[1]),
        pltpu.make_async_copy(pos_hbm, pos_ref, load_s.at[2]),
    ]
    for j in range(emb // chunk):
        at = slice(j * chunk, (j + 1) * chunk)
        loads.append(pltpu.make_async_copy(w_hbm.at[:, at], w_ref.at[:, at], load_s.at[3 + j]))
    for c in loads:
        c.start()

    barrier = pltpu.get_barrier_semaphore()
    for k in range(1, plane):
        pl.semaphore_signal(barrier, inc=1, device_id=in_plane(k)[1], device_id_type=MESH)
    for k in range(1, blocks):
        pl.semaphore_signal(barrier, inc=1, device_id=along(k)[1], device_id_type=MESH)

    loads[0].wait()
    hid_all[z] = hid_ref[...].T
    loads[1].wait()
    text = txt_ref[...].astype(F32)
    txt[slot(z, texts), :] = (text / row_norm(text)).astype(BF16)
    pl.semaphore_wait(barrier, plane - 1 + blocks - 1)
    line_send(0, text_at, txt_s, txt_r)
    mine = hid_all[z, slot(g, band), :]
    for j in range(emb // chunk):
        at = slice(j * chunk, (j + 1) * chunk)
        loads[3 + j].wait()
        own_part[:, at] = jnp.dot(mine, w_ref[:, at], preferred_element_type=F32)
        for k in range(1, splits):
            q = lax.rem(x + k, splits)
            send(own_part.at[slot(q, own), at], part_recv.at[slot(x, own), at],
                 part_s.at[j, k], part_r.at[j, k], (g, z, q))
    loads[2].wait()
    line_land(0, text_at, txt_s, txt_r)
    line_send(1, text_at, txt_s, txt_r)
    line_send(0, hid_at, hid_s, hid_r)

    emb_rows = own_part[slot(x, own), :]
    for k in range(1, splits):
        q = lax.rem(x + splits - k, splits)
        there = part_recv.at[slot(q, own), :]
        for j in range(emb // chunk):
            piece = part_recv.at[slot(q, own), j * chunk:(j + 1) * chunk]
            landed(piece, part_s.at[j, k], part_r.at[j, k], (g, z, q))
        emb_rows = emb_rows + there[...]
    norm = row_norm(emb_rows)
    unit = emb_rows / norm
    unit_ref[...] = unit
    norm_ref[...] = jnp.broadcast_to(norm, norm_ref.shape)
    img[slot(p, own), :] = unit.astype(BF16)
    gather_start(img, img_s, img_r)

    line_land(1, text_at, txt_s, txt_r)
    line_send(2, text_at, txt_s, txt_r)
    gather_finish(img, img_s, img_r)
    for step in range(2, blocks - 1):
        line_land(step, text_at, txt_s, txt_r)
        line_send(step + 1, text_at, txt_s, txt_r)

    count = blocks * texts
    sims = lax.dot_general(
        txt[...], img[...], (((1,), (1,)), ((), ())), preferred_element_type=F32
    )
    scale = jnp.exp(temp_ref[...])
    logits = scale * sims + bias_ref[...]
    at = lax.broadcasted_iota(jnp.int32, (count, 1), 0)
    column = at + (g * blocks * splits + x) * texts
    for j in range(1, blocks):
        column = column + jnp.where(at >= j * texts, (splits - 1) * texts, 0)
    match = column == pos_ref[...]
    signed = jnp.where(match, logits, -logits)
    small = jnp.exp(-jnp.abs(signed))
    loss_at = jnp.log1p(small) - jnp.minimum(signed, 0.0)
    slope = jnp.where(signed >= 0.0, small, 1.0) / (1.0 + small)
    slope = jnp.where(match, -slope, slope)
    wts[...] = (scale * slope).astype(BF16)

    for j in range(emb // chunk):
        c = slice(j * chunk, (j + 1) * chunk)
        gi_own[:, c] = lax.dot_general(
            wts[...], txt[:, c], (((0,), (0,)), ((), ())), preferred_element_type=F32
        )
    if pair == 2:
        for o in range(outer):
            send(gi_own.at[slot(o * pair + 1 - half, band), :], gi_pair.at[o],
                 gp_s.at[o], gp_r.at[o], sibling)

    hid_land(0)
    line_send(1, hid_at, hid_s, hid_r)
    for j in range(emb // chunk):
        c = slice(j * chunk, (j + 1) * chunk)
        value = jnp.dot(wts[...], img[:, c], preferred_element_type=F32)
        gt_send[:, c] = value.astype(BF16)
        gt_own[:, c] = value
    for o in range(outer):
        value = gi_own[slot(o * pair + half, band), :]
        if pair == 2:
            landed(gi_pair.at[o], gp_s.at[o], gp_r.at[o], sibling)
            value = value + gi_pair[o]
            gi_pair[o] = value
        gi_send[slot(o, band), :] = value.astype(BF16)
    for k in range(1, chips):
        c = to_chip(k)
        send(gi_send.at[slot(c, own), :], gi_recv.at[slot(chip, own), :],
             gi_s.at[k], gi_r.at[k], chip_device(c))

    def add_all(v):
        return jnp.sum(jnp.sum(v, axis=1, keepdims=True), axis=0, keepdims=True)

    line = lax.broadcasted_iota(jnp.int32, (8, LANES), 0)
    stat = jnp.where(line == 0, add_all(loss_at), 0.0)
    stat = jnp.where(line == 1, add_all(slope * sims), stat)
    stat = jnp.where(line == 2, add_all(slope), stat)
    stat_plane[p] = stat
    for k in range(1, plane):
        here = stat_plane.at[p]
        send(here, here, sp_s.at[k], sp_r.at[k], in_plane(k)[1])

    hid_land(1)
    line_send(2, hid_at, hid_s, hid_r)
    if pair == 2:
        grads = gi_pair[out, slot(x, own), :]
    else:
        grads = gi_own[slot(p, own), :]
    for k in range(1, chips):
        there = gi_recv.at[slot(from_chip(k), own), :]
        landed(there, gi_s.at[k], gi_r.at[k], chip_device(from_chip(k)))
        grads = grads + there[...].astype(F32)
    rounded = unit_backward(grads, unit_ref[...], norm_ref[:, :1]).astype(BF16)
    low[slot(p, own), :] = rounded
    for j in range(blocks):
        for i in range(groups):
            at = i * group_cols + j * cols
            col_send[j, :, i * width:i * width + cols] = rounded[:, at:at + cols]
    for k in range(1, blocks):
        q, device = along(k)
        send(col_send.at[q], col_mid.at[z], cz_s.at[k], cz_r.at[k], device)
    gather_start(low, low_s, low_r)
    for k in range(1, blocks):
        q, device = along(k)
        send(gt_send.at[slot(q, texts), :], gt_recv.at[slot(z, texts), :],
             gt_s.at[k], gt_r.at[k], device)
    col_mid[z] = col_send[z]

    for k in range(1, blocks):
        landed(col_mid.at[from_along(k)], cz_s.at[k], cz_r.at[k], along(k)[1])
    for k in range(1, plane):
        q, device = in_plane(k)
        send(col_mid.at[:, :, slot(lax.div(q, splits), width)],
             col_all.at[:, slot(p, own), :], cp_s.at[k], cp_r.at[k], device)
    col_all[:, slot(p, own), :] = col_mid[:, :, slot(g, width)]
    for k in range(1, plane):
        there = stat_plane.at[from_plane(k)]
        landed(there, sp_s.at[k], sp_r.at[k], in_plane(k)[1])
    stat = stat_plane[0]
    for j in range(1, plane):
        stat = stat + stat_plane[j]
    stat_all[z] = stat
    for k in range(1, blocks):
        here = stat_all.at[z]
        send(here, here, sa_s.at[k], sa_r.at[k], along(k)[1])
    gather_finish(low, low_s, low_r)
    for step in range(2, blocks - 1):
        hid_land(step)
        line_send(step + 1, hid_at, hid_s, hid_r)
    stores = [pltpu.make_async_copy(low, gimg_hbm, store_s.at[0])]
    stores[-1].start()

    for k in range(1, blocks):
        there = stat_all.at[from_along(k)]
        landed(there, sa_s.at[k], sa_r.at[k], along(k)[1])
    stat = stat_all[0]
    for j in range(1, blocks):
        stat = stat + stat_all[j]
    stat_ref[...] = jnp.where(line == 1, scale * stat, stat) / pairs

    if pair == 2:
        for k in range(1, blocks):
            q = from_along(k)
            there = hid_all.at[q, slot(1 - half, part_rows), :]
            landed(there, hp_s.at[q], hp_r.at[q], sibling)
            hid_pair(q).wait_send()
    for k in range(1, plane):
        there = col_all.at[:, slot(from_plane(k), own), :]
        landed(there, cp_s.at[k], cp_r.at[k], in_plane(k)[1])
    total[...] = jnp.zeros_like(total)
    for q in range(blocks):
        total[...] += lax.dot_general(
            col_all[q], hid_all[q], (((0,), (0,)), ((), ())), preferred_element_type=F32
        )
    gw_ref[...] = total[0:cols, :]
    stores.append(pltpu.make_async_copy(gw_ref, gw_hbm, store_s.at[2]))
    stores[-1].start()

    grads = gt_own[slot(z, texts), :]
    for k in range(1, blocks):
        there = gt_recv.at[slot(from_along(k), texts), :]
        landed(there, gt_s.at[k], gt_r.at[k], along(k)[1])
        grads = grads + there[...].astype(F32)
    text = txt_ref[...].astype(F32)
    norm = row_norm(text)
    gtxt_ref[...] = unit_backward(grads, text / norm, norm)
    stores.append(pltpu.make_async_copy(gtxt_ref, gtxt_hbm, store_s.at[1]))
    stores[-1].start()

    line_sent(text_at, txt_s, txt_r)
    line_sent(hid_at, hid_s, hid_r)
    for c in sent:
        c.wait_send()
    for c in stores:
        c.wait()


def finish(parts, stat_ref, low_hbm, txt_hbm, w_hbm, loss_ref, gtemp_ref, gbias_ref,
           gimg_hbm, gtxt_hbm, gw_hbm, low, wide, txt, wgt, sem_in, sem_out):
    size = low.shape[0] // parts
    cuts = [slice(j * size, (j + 1) * size) for j in range(parts)]
    loads = [
        pltpu.make_async_copy(low_hbm.at[c, :], low.at[c, :], sem_in.at[j])
        for j, c in enumerate(cuts)
    ]
    loads.append(pltpu.make_async_copy(txt_hbm, txt, sem_in.at[parts]))
    loads.append(pltpu.make_async_copy(w_hbm, wgt, sem_in.at[parts + 1]))
    for c in loads:
        c.start()
    stores = []
    loss_ref[...] = stat_ref[0:1, 0:1]
    gtemp_ref[...] = stat_ref[1:2, 0:1]
    gbias_ref[...] = stat_ref[2:3, 0:1]
    for j, c in enumerate(cuts):
        loads[j].wait()
        wide[c, :] = low[c, :].astype(F32)
        done = pltpu.make_async_copy(wide.at[c, :], gimg_hbm.at[c, :], sem_out.at[j])
        done.start()
        stores.append(done)
    for j, (buf, out) in enumerate(((txt, gtxt_hbm), (wgt, gw_hbm))):
        loads[parts + j].wait()
        done = pltpu.make_async_copy(buf, out, sem_out.at[parts + j])
        done.start()
        stores.append(done)
    for c in stores:
        c.wait()


def on_device(image_hidden, image_weight, text_embed, positives, log_temp, bias):
    groups, blocks, splits = (lax.axis_size(a) for a in ("group", "blk", "mp"))
    plane = groups * splits
    rows, depth = image_hidden.shape
    emb = image_weight.shape[1]
    texts = text_embed.shape[0]
    own = rows // plane
    pair = 2 if groups % 2 == 0 else 1
    band = splits * own
    count = blocks * texts
    cols = emb // (groups * blocks)
    width = -(-cols // LANES) * LANES
    vmem = pl.BlockSpec(memory_space=pltpu.VMEM)
    anywhere = pl.BlockSpec(memory_space=pl.ANY)
    dma = pltpu.SemaphoreType.DMA
    outs = pl.pallas_call(
        functools.partial(kernel, (groups, blocks, splits)),
        out_shape=[
            jax.ShapeDtypeStruct((8, LANES), F32),
            jax.ShapeDtypeStruct((rows, emb), BF16),
            jax.ShapeDtypeStruct((texts, emb), F32),
            jax.ShapeDtypeStruct((cols, depth), F32),
        ],
        in_specs=[anywhere] * 4 + [vmem] * 2,
        out_specs=[vmem] + [anywhere] * 3,
        scratch_shapes=[
            pltpu.VMEM((depth, rows), BF16),
            pltpu.VMEM((depth, emb), BF16),
            pltpu.VMEM((texts, emb), BF16),
            pltpu.VMEM((1, rows), jnp.int32),
            pltpu.VMEM((band, emb), F32),
            pltpu.VMEM((band, emb), F32),
            pltpu.VMEM((own, emb), F32),
            pltpu.VMEM((own, LANES), F32),
            pltpu.VMEM((rows, emb), BF16),
            pltpu.VMEM((count, emb), BF16),
            pltpu.VMEM((blocks, rows, depth), BF16),
            pltpu.VMEM((count, rows), BF16),
            pltpu.VMEM((rows, emb), F32),
            pltpu.VMEM((rows // pair // band, band, emb), F32),
            pltpu.VMEM((rows // pair, emb), BF16),
            pltpu.VMEM((rows // pair, emb), BF16),
            pltpu.VMEM((rows, emb), BF16),
            pltpu.VMEM((count, emb), BF16),
            pltpu.VMEM((count, emb), BF16),
            pltpu.VMEM((count, emb), F32),
            pltpu.VMEM((blocks, own, groups * width), BF16),
            pltpu.VMEM((blocks, own, groups * width), BF16),
            pltpu.VMEM((blocks, rows, width), BF16),
            pltpu.VMEM((plane, 8, LANES), F32),
            pltpu.VMEM((blocks, 8, LANES), F32),
            pltpu.VMEM((width, depth), F32),
            pltpu.VMEM((texts, emb), F32),
            pltpu.VMEM((cols, depth), F32),
            dma((3 + groups,)),
            dma((3,)),
            dma((groups, splits)), dma((groups, splits)),
            dma((plane,)), dma((plane,)),
            dma((2 * blocks,)), dma((2 * blocks,)),
            dma((2 * blocks,)), dma((2 * blocks,)),
            dma((blocks,)), dma((blocks,)),
            dma((groups,)), dma((groups,)),
            dma((plane,)), dma((plane,)),
            dma((plane,)), dma((plane,)),
            dma((blocks,)), dma((blocks,)),
            dma((blocks,)), dma((blocks,)),
            dma((plane,)), dma((plane,)),
            dma((plane,)), dma((plane,)),
            dma((blocks,)), dma((blocks,)),
        ],
        compiler_params=pltpu.CompilerParams(
            collective_id=0, has_side_effects=True, vmem_limit_bytes=LIMIT
        ),
        name="contrast",
    )(
        image_hidden.T, image_weight, text_embed, positives.reshape(1, rows),
        log_temp.reshape(1, 1), bias.reshape(1, 1),
    )
    parts = 4 if rows % 64 == 0 else 1
    loss, grad_temp, grad_bias, grad_image, grad_text, grad_weight = pl.pallas_call(
        functools.partial(finish, parts),
        out_shape=[
            jax.ShapeDtypeStruct((1, 1), F32),
            jax.ShapeDtypeStruct((1, 1), F32),
            jax.ShapeDtypeStruct((1, 1), F32),
            jax.ShapeDtypeStruct((rows, emb), F32),
            jax.ShapeDtypeStruct((texts, emb), F32),
            jax.ShapeDtypeStruct((cols, depth), F32),
        ],
        in_specs=[vmem] + [anywhere] * 3,
        out_specs=[vmem] * 3 + [anywhere] * 3,
        scratch_shapes=[
            pltpu.VMEM((rows, emb), BF16),
            pltpu.VMEM((rows, emb), F32),
            pltpu.VMEM((texts, emb), F32),
            pltpu.VMEM((cols, depth), F32),
            dma((parts + 2,)),
            dma((parts + 2,)),
        ],
        compiler_params=pltpu.CompilerParams(vmem_limit_bytes=LIMIT),
        name="finish",
    )(*outs)
    return (
        loss.reshape(1), grad_temp.reshape(1), grad_bias.reshape(1),
        grad_image, grad_text, grad_weight.T,
    )


def solution(mesh):
    in_specs = (P("blk", "mp"), P("mp", None), P(("group", "blk", "mp"), None), P("blk"), P(), P())
    out_specs = (
        P(),
        P(),
        P(),
        P("blk", None),
        P(("group", "blk", "mp"), None),
        P("mp", ("group", "blk")),
    )
    return jax.shard_map(
        on_device, mesh=mesh, in_specs=in_specs, out_specs=out_specs, check_vma=False
    )
```

```python
import functools

import jax
import jax.numpy as jnp
from jax import lax
from jax.experimental import pallas as pl
from jax.experimental.pallas import tpu as pltpu
from jax.sharding import PartitionSpec as P

MESH = pl.DeviceIdType.MESH
LANES = 128
LIMIT = 64 * 1024 * 1024 - 64 * 1024
F32 = jnp.float32
BF16 = jnp.bfloat16


def row_norm(values):
    return jnp.sqrt(jnp.sum(values * values, axis=1, keepdims=True) + 1e-06)


def unit_backward(grads, unit, norm_rows):
    return (grads - unit * jnp.sum(unit * grads, axis=1, keepdims=True)) / norm_rows


def kernel(
    sizes,
    hid_hbm, w_hbm, txt_hbm, pos_hbm, temp_ref, bias_ref,
    stat_ref, gimg_hbm, gtxt_hbm, gw_hbm,
    hid_ref, w_ref, txt_ref, pos_ref, part_recv, own_part, unit_ref, norm_ref, img, txt, hid_all,
    wts, gi_own, gi_pair, gi_send, gi_recv, low, gt_send, gt_recv, gt_own,
    col_send, col_mid, col_all, stat_plane, stat_all, total,
    gtxt_ref, gw_ref, load_s, store_s, part_s, part_r, img_s, img_r, txt_s, txt_r, hid_s, hid_r, hp_s, hp_r, gp_s, gp_r, gi_s, gi_r,
    low_s, low_r, gt_s, gt_r, cz_s, cz_r, cp_s, cp_r, sp_s, sp_r, sa_s, sa_r,
):
    groups, blocks, splits = sizes
    plane = groups * splits
    pair = 2 if groups % 2 == 0 else 1
    outer = groups // pair
    chips = outer * splits
    rows, emb = img.shape
    own = rows // plane
    band = splits * own
    texts = txt_ref.shape[0]
    pairs = rows * blocks
    group_cols = emb // groups
    cols = group_cols // blocks
    width = total.shape[0]
    part_rows = rows // pair
    chunk = group_cols
    g, z, x = lax.axis_index("group"), lax.axis_index("blk"), lax.axis_index("mp")
    p = g * splits + x
    half, out = lax.rem(g, pair), lax.div(g, pair)
    chip = out * splits + x
    sibling = (out * pair + (pair - 1 - half), z, x)

    def in_plane(k):
        q = lax.rem(p + k, plane)
        return q, (lax.div(q, splits), z, lax.rem(q, splits))

    def from_plane(k):
        return lax.rem(p + plane - k, plane)

    def on_chip(c, h):
        return (lax.div(c, splits) * pair + h) * splits + lax.rem(c, splits)

    def chip_device(c):
        return (lax.div(c, splits) * pair + half, z, lax.rem(c, splits))

    def to_chip(k):
        return lax.rem(chip + k, chips)

    def from_chip(k):
        return lax.rem(chip + chips - k, chips)

    def along(k):
        q = lax.rem(z + k, blocks)
        return q, (g, q, x)

    def from_along(k):
        return lax.rem(z + blocks - k, blocks)

    def slot(i, size):
        return pl.ds(pl.multiple_of(i * size, size), size)

    def copy(src, dst, send_sem, recv_sem, device):
        return pltpu.make_async_remote_copy(
            src_ref=src, dst_ref=dst, send_sem=send_sem, recv_sem=recv_sem,
            device_id=device, device_id_type=MESH,
        )

    sent = []

    def send(*args):
        c = copy(*args)
        c.start()
        sent.append(c)

    def landed(dst, send_sem, recv_sem, device):
        copy(dst, dst, send_sem, recv_sem, device).wait_recv()

    def gather_start(buf, s_sem, r_sem):
        here = buf.at[slot(p, own), :]
        for k in range(1, chips):
            send(here, here, s_sem.at[k], r_sem.at[k], chip_device(to_chip(k)))
        if pair == 2:
            send(here, here, s_sem.at[chips], r_sem.at[chips], sibling)

    def gather_finish(buf, s_sem, r_sem):
        for k in range(1, chips):
            there = buf.at[slot(on_chip(from_chip(k), half), own), :]
            landed(there, s_sem.at[k], r_sem.at[k], chip_device(from_chip(k)))
            if pair == 2:
                send(there, there, s_sem.at[chips + k], r_sem.at[chips + k], sibling)
        if pair == 2:
            for k in range(chips):
                there = buf.at[slot(on_chip(from_chip(k), 1 - half), own), :]
                landed(there, s_sem.at[chips + k], r_sem.at[chips + k], sibling)

    def line_copies(step, at, s_sem, r_sem):
        up = copy(at(z - step), at(z - step), s_sem.at[step], r_sem.at[step], (g, z + 1, x))
        down = copy(at(z + step), at(z + step), s_sem.at[blocks + step],
                    r_sem.at[blocks + step], (g, z - 1, x))
        return (((z - step >= 0) & (z + 1 < blocks), up),
                ((z + step < blocks) & (z - 1 >= 0), down))

    def line_send(step, at, s_sem, r_sem):
        if step < blocks - 1:
            for held, c in line_copies(step, at, s_sem, r_sem):
                pl.when(held)(c.start)

    def line_sent(at, s_sem, r_sem):
        for step in range(blocks - 1):
            for held, c in line_copies(step, at, s_sem, r_sem):
                pl.when(held)(c.wait_send)

    def line_land(step, at, s_sem, r_sem, then=None):
        if step >= blocks - 1:
            return
        for came, q, i, device in (
            (z - 1 - step >= 0, z - 1 - step, step, (g, z - 1, x)),
            (z + 1 + step < blocks, z + 1 + step, blocks + step, (g, z + 1, x)),
        ):
            @pl.when(came)
            def _():
                landed(at(q), s_sem.at[i], r_sem.at[i], device)
                if then is not None:
                    then(q)

    def text_at(q):
        return txt.at[slot(q, texts), :]

    def hid_at(q):
        return hid_all.at[q, slot(half, part_rows), :]

    def hid_pair(q):
        return copy(hid_at(q), hid_at(q), hp_s.at[q], hp_r.at[q], sibling)

    def hid_land(step):
        line_land(step, hid_at, hid_s, hid_r,
                  (lambda q: hid_pair(q).start()) if pair == 2 else None)

    loads = [
        pltpu.make_async_copy(hid_hbm, hid_ref, load_s.at[0]),
        pltpu.make_async_copy(txt_hbm, txt_ref, load_s.at[1]),
        pltpu.make_async_copy(pos_hbm, pos_ref, load_s.at[2]),
    ]
    for j in range(emb // chunk):
        at = slice(j * chunk, (j + 1) * chunk)
        loads.append(pltpu.make_async_copy(w_hbm.at[:, at], w_ref.at[:, at], load_s.at[3 + j]))
    for c in loads:
        c.start()

    barrier = pltpu.get_barrier_semaphore()
    for k in range(1, plane):
        pl.semaphore_signal(barrier, inc=1, device_id=in_plane(k)[1], device_id_type=MESH)
    for k in range(1, blocks):
        pl.semaphore_signal(barrier, inc=1, device_id=along(k)[1], device_id_type=MESH)

    loads[0].wait()
    hid_all[z] = hid_ref[...].T
    loads[1].wait()
    text = txt_ref[...].astype(F32)
    txt[slot(z, texts), :] = (text / row_norm(text)).astype(BF16)
    pl.semaphore_wait(barrier, plane - 1 + blocks - 1)
    line_send(0, text_at, txt_s, txt_r)
    mine = hid_all[z, slot(g, band), :]
    for j in range(emb // chunk):
        at = slice(j * chunk, (j + 1) * chunk)
        loads[3 + j].wait()
        own_part[:, at] = jnp.dot(mine, w_ref[:, at], preferred_element_type=F32)
        for k in range(1, splits):
            q = lax.rem(x + k, splits)
            send(own_part.at[slot(q, own), at], part_recv.at[slot(x, own), at],
                 part_s.at[j, k], part_r.at[j, k], (g, z, q))
    loads[2].wait()
    line_land(0, text_at, txt_s, txt_r)
    line_send(1, text_at, txt_s, txt_r)
    line_send(0, hid_at, hid_s, hid_r)

    emb_rows = own_part[slot(x, own), :]
    for k in range(1, splits):
        q = lax.rem(x + splits - k, splits)
        there = part_recv.at[slot(q, own), :]
        for j in range(emb // chunk):
            piece = part_recv.at[slot(q, own), j * chunk:(j + 1) * chunk]
            landed(piece, part_s.at[j, k], part_r.at[j, k], (g, z, q))
        emb_rows = emb_rows + there[...]
    norm = row_norm(emb_rows)
    unit = emb_rows / norm
    unit_ref[...] = unit
    norm_ref[...] = jnp.broadcast_to(norm, norm_ref.shape)
    img[slot(p, own), :] = unit.astype(BF16)
    gather_start(img, img_s, img_r)

    line_land(1, text_at, txt_s, txt_r)
    line_send(2, text_at, txt_s, txt_r)
    gather_finish(img, img_s, img_r)
    for step in range(2, blocks - 1):
        line_land(step, text_at, txt_s, txt_r)
        line_send(step + 1, text_at, txt_s, txt_r)

    count = blocks * texts
    sims = lax.dot_general(
        txt[...], img[...], (((1,), (1,)), ((), ())), preferred_element_type=F32
    )
    scale = jnp.exp(temp_ref[...])
    logits = scale * sims + bias_ref[...]
    at = lax.broadcasted_iota(jnp.int32, (count, 1), 0)
    column = at + (g * blocks * splits + x) * texts
    for j in range(1, blocks):
        column = column + jnp.where(at >= j * texts, (splits - 1) * texts, 0)
    match = column == pos_ref[...]
    signed = jnp.where(match, logits, -logits)
    small = jnp.exp(-jnp.abs(signed))
    loss_at = jnp.log1p(small) - jnp.minimum(signed, 0.0)
    slope = jnp.where(signed >= 0.0, small, 1.0) / (1.0 + small)
    slope = jnp.where(match, -slope, slope)
    wts[...] = (scale * slope).astype(BF16)

    for j in range(emb // chunk):
        c = slice(j * chunk, (j + 1) * chunk)
        gi_own[:, c] = lax.dot_general(
            wts[...], txt[:, c], (((0,), (0,)), ((), ())), preferred_element_type=F32
        )
        if pair == 2:
            for o in range(outer):
                send(gi_own.at[slot(o * pair + 1 - half, band), c], gi_pair.at[o, :, c],
                     gp_s.at[o, j], gp_r.at[o, j], sibling)

    hid_land(0)
    line_send(1, hid_at, hid_s, hid_r)
    for j in range(emb // chunk):
        c = slice(j * chunk, (j + 1) * chunk)
        value = jnp.dot(wts[...], img[:, c], preferred_element_type=F32)
        gt_send[:, c] = value.astype(BF16)
        gt_own[:, c] = value
    for o in range(outer):
        value = gi_own[slot(o * pair + half, band), :]
        if pair == 2:
            for j in range(emb // chunk):
                piece = gi_pair.at[o, :, j * chunk:(j + 1) * chunk]
                landed(piece, gp_s.at[o, j], gp_r.at[o, j], sibling)
            value = value + gi_pair[o]
            gi_pair[o] = value
        gi_send[slot(o, band), :] = value.astype(BF16)
    for k in range(1, chips):
        c = to_chip(k)
        send(gi_send.at[slot(c, own), :], gi_recv.at[slot(chip, own), :],
             gi_s.at[k], gi_r.at[k], chip_device(c))

    def add_all(v):
        return jnp.sum(jnp.sum(v, axis=1, keepdims=True), axis=0, keepdims=True)

    line = lax.broadcasted_iota(jnp.int32, (8, LANES), 0)
    stat = jnp.where(line == 0, add_all(loss_at), 0.0)
    stat = jnp.where(line == 1, add_all(slope * sims), stat)
    stat = jnp.where(line == 2, add_all(slope), stat)
    stat_plane[p] = stat
    for k in range(1, plane):
        here = stat_plane.at[p]
        send(here, here, sp_s.at[k], sp_r.at[k], in_plane(k)[1])

    hid_land(1)
    line_send(2, hid_at, hid_s, hid_r)
    if pair == 2:
        grads = gi_pair[out, slot(x, own), :]
    else:
        grads = gi_own[slot(p, own), :]
    for k in range(1, chips):
        there = gi_recv.at[slot(from_chip(k), own), :]
        landed(there, gi_s.at[k], gi_r.at[k], chip_device(from_chip(k)))
        grads = grads + there[...].astype(F32)
    rounded = unit_backward(grads, unit_ref[...], norm_ref[:, :1]).astype(BF16)
    low[slot(p, own), :] = rounded
    for j in range(blocks):
        for i in range(groups):
            at = i * group_cols + j * cols
            col_send[j, :, i * width:i * width + cols] = rounded[:, at:at + cols]
    for k in range(1, blocks):
        q, device = along(k)
        send(col_send.at[q], col_mid.at[z], cz_s.at[k], cz_r.at[k], device)
    gather_start(low, low_s, low_r)
    for k in range(1, blocks):
        q, device = along(k)
        send(gt_send.at[slot(q, texts), :], gt_recv.at[slot(z, texts), :],
             gt_s.at[k], gt_r.at[k], device)
    col_mid[z] = col_send[z]

    for k in range(1, blocks):
        landed(col_mid.at[from_along(k)], cz_s.at[k], cz_r.at[k], along(k)[1])
    for k in range(1, plane):
        q, device = in_plane(k)
        send(col_mid.at[:, :, slot(lax.div(q, splits), width)],
             col_all.at[:, slot(p, own), :], cp_s.at[k], cp_r.at[k], device)
    col_all[:, slot(p, own), :] = col_mid[:, :, slot(g, width)]
    for k in range(1, plane):
        there = stat_plane.at[from_plane(k)]
        landed(there, sp_s.at[k], sp_r.at[k], in_plane(k)[1])
    stat = stat_plane[0]
    for j in range(1, plane):
        stat = stat + stat_plane[j]
    stat_all[z] = stat
    for k in range(1, blocks):
        here = stat_all.at[z]
        send(here, here, sa_s.at[k], sa_r.at[k], along(k)[1])
    gather_finish(low, low_s, low_r)
    for step in range(2, blocks - 1):
        hid_land(step)
        line_send(step + 1, hid_at, hid_s, hid_r)
    stores = [pltpu.make_async_copy(low, gimg_hbm, store_s.at[0])]
    stores[-1].start()

    for k in range(1, blocks):
        there = stat_all.at[from_along(k)]
        landed(there, sa_s.at[k], sa_r.at[k], along(k)[1])
    stat = stat_all[0]
    for j in range(1, blocks):
        stat = stat + stat_all[j]
    stat_ref[...] = jnp.where(line == 1, scale * stat, stat) / pairs

    if pair == 2:
        for k in range(1, blocks):
            q = from_along(k)
            there = hid_all.at[q, slot(1 - half, part_rows), :]
            landed(there, hp_s.at[q], hp_r.at[q], sibling)
            hid_pair(q).wait_send()
    for k in range(1, plane):
        there = col_all.at[:, slot(from_plane(k), own), :]
        landed(there, cp_s.at[k], cp_r.at[k], in_plane(k)[1])
    total[...] = jnp.zeros_like(total)
    for q in range(blocks):
        total[...] += lax.dot_general(
            col_all[q], hid_all[q], (((0,), (0,)), ((), ())), preferred_element_type=F32
        )
    gw_ref[...] = total[0:cols, :]
    stores.append(pltpu.make_async_copy(gw_ref, gw_hbm, store_s.at[2]))
    stores[-1].start()

    grads = gt_own[slot(z, texts), :]
    for k in range(1, blocks):
        there = gt_recv.at[slot(from_along(k), texts), :]
        landed(there, gt_s.at[k], gt_r.at[k], along(k)[1])
        grads = grads + there[...].astype(F32)
    text = txt_ref[...].astype(F32)
    norm = row_norm(text)
    gtxt_ref[...] = unit_backward(grads, text / norm, norm)
    stores.append(pltpu.make_async_copy(gtxt_ref, gtxt_hbm, store_s.at[1]))
    stores[-1].start()

    line_sent(text_at, txt_s, txt_r)
    line_sent(hid_at, hid_s, hid_r)
    for c in sent:
        c.wait_send()
    for c in stores:
        c.wait()


def finish(parts, stat_ref, low_hbm, txt_hbm, w_hbm, loss_ref, gtemp_ref, gbias_ref,
           gimg_hbm, gtxt_hbm, gw_hbm, low, wide, txt, wgt, sem_in, sem_out):
    size = low.shape[0] // parts
    cuts = [slice(j * size, (j + 1) * size) for j in range(parts)]
    loads = [
        pltpu.make_async_copy(low_hbm.at[c, :], low.at[c, :], sem_in.at[j])
        for j, c in enumerate(cuts)
    ]
    loads.append(pltpu.make_async_copy(txt_hbm, txt, sem_in.at[parts]))
    loads.append(pltpu.make_async_copy(w_hbm, wgt, sem_in.at[parts + 1]))
    for c in loads:
        c.start()
    stores = []
    loss_ref[...] = stat_ref[0:1, 0:1]
    gtemp_ref[...] = stat_ref[1:2, 0:1]
    gbias_ref[...] = stat_ref[2:3, 0:1]
    for j, c in enumerate(cuts):
        loads[j].wait()
        wide[c, :] = low[c, :].astype(F32)
        done = pltpu.make_async_copy(wide.at[c, :], gimg_hbm.at[c, :], sem_out.at[j])
        done.start()
        stores.append(done)
    for j, (buf, out) in enumerate(((txt, gtxt_hbm), (wgt, gw_hbm))):
        loads[parts + j].wait()
        done = pltpu.make_async_copy(buf, out, sem_out.at[parts + j])
        done.start()
        stores.append(done)
    for c in stores:
        c.wait()


def on_device(image_hidden, image_weight, text_embed, positives, log_temp, bias):
    groups, blocks, splits = (lax.axis_size(a) for a in ("group", "blk", "mp"))
    plane = groups * splits
    rows, depth = image_hidden.shape
    emb = image_weight.shape[1]
    texts = text_embed.shape[0]
    own = rows // plane
    pair = 2 if groups % 2 == 0 else 1
    band = splits * own
    count = blocks * texts
    cols = emb // (groups * blocks)
    width = -(-cols // LANES) * LANES
    vmem = pl.BlockSpec(memory_space=pltpu.VMEM)
    anywhere = pl.BlockSpec(memory_space=pl.ANY)
    dma = pltpu.SemaphoreType.DMA
    outs = pl.pallas_call(
        functools.partial(kernel, (groups, blocks, splits)),
        out_shape=[
            jax.ShapeDtypeStruct((8, LANES), F32),
            jax.ShapeDtypeStruct((rows, emb), BF16),
            jax.ShapeDtypeStruct((texts, emb), F32),
            jax.ShapeDtypeStruct((cols, depth), F32),
        ],
        in_specs=[anywhere] * 4 + [vmem] * 2,
        out_specs=[vmem] + [anywhere] * 3,
        scratch_shapes=[
            pltpu.VMEM((depth, rows), BF16),
            pltpu.VMEM((depth, emb), BF16),
            pltpu.VMEM((texts, emb), BF16),
            pltpu.VMEM((1, rows), jnp.int32),
            pltpu.VMEM((band, emb), F32),
            pltpu.VMEM((band, emb), F32),
            pltpu.VMEM((own, emb), F32),
            pltpu.VMEM((own, LANES), F32),
            pltpu.VMEM((rows, emb), BF16),
            pltpu.VMEM((count, emb), BF16),
            pltpu.VMEM((blocks, rows, depth), BF16),
            pltpu.VMEM((count, rows), BF16),
            pltpu.VMEM((rows, emb), F32),
            pltpu.VMEM((rows // pair // band, band, emb), F32),
            pltpu.VMEM((rows // pair, emb), BF16),
            pltpu.VMEM((rows // pair, emb), BF16),
            pltpu.VMEM((rows, emb), BF16),
            pltpu.VMEM((count, emb), BF16),
            pltpu.VMEM((count, emb), BF16),
            pltpu.VMEM((count, emb), F32),
            pltpu.VMEM((blocks, own, groups * width), BF16),
            pltpu.VMEM((blocks, own, groups * width), BF16),
            pltpu.VMEM((blocks, rows, width), BF16),
            pltpu.VMEM((plane, 8, LANES), F32),
            pltpu.VMEM((blocks, 8, LANES), F32),
            pltpu.VMEM((width, depth), F32),
            pltpu.VMEM((texts, emb), F32),
            pltpu.VMEM((cols, depth), F32),
            dma((3 + groups,)),
            dma((3,)),
            dma((groups, splits)), dma((groups, splits)),
            dma((plane,)), dma((plane,)),
            dma((2 * blocks,)), dma((2 * blocks,)),
            dma((2 * blocks,)), dma((2 * blocks,)),
            dma((blocks,)), dma((blocks,)),
            dma((groups, groups)), dma((groups, groups)),
            dma((plane,)), dma((plane,)),
            dma((plane,)), dma((plane,)),
            dma((blocks,)), dma((blocks,)),
            dma((blocks,)), dma((blocks,)),
            dma((plane,)), dma((plane,)),
            dma((plane,)), dma((plane,)),
            dma((blocks,)), dma((blocks,)),
        ],
        compiler_params=pltpu.CompilerParams(
            collective_id=0, has_side_effects=True, vmem_limit_bytes=LIMIT
        ),
        name="contrast",
    )(
        image_hidden.T, image_weight, text_embed, positives.reshape(1, rows),
        log_temp.reshape(1, 1), bias.reshape(1, 1),
    )
    parts = 4 if rows % 64 == 0 else 1
    loss, grad_temp, grad_bias, grad_image, grad_text, grad_weight = pl.pallas_call(
        functools.partial(finish, parts),
        out_shape=[
            jax.ShapeDtypeStruct((1, 1), F32),
            jax.ShapeDtypeStruct((1, 1), F32),
            jax.ShapeDtypeStruct((1, 1), F32),
            jax.ShapeDtypeStruct((rows, emb), F32),
            jax.ShapeDtypeStruct((texts, emb), F32),
            jax.ShapeDtypeStruct((cols, depth), F32),
        ],
        in_specs=[vmem] + [anywhere] * 3,
        out_specs=[vmem] * 3 + [anywhere] * 3,
        scratch_shapes=[
            pltpu.VMEM((rows, emb), BF16),
            pltpu.VMEM((rows, emb), F32),
            pltpu.VMEM((texts, emb), F32),
            pltpu.VMEM((cols, depth), F32),
            dma((parts + 2,)),
            dma((parts + 2,)),
        ],
        compiler_params=pltpu.CompilerParams(vmem_limit_bytes=LIMIT),
        name="finish",
    )(*outs)
    return (
        loss.reshape(1), grad_temp.reshape(1), grad_bias.reshape(1),
        grad_image, grad_text, grad_weight.T,
    )


def solution(mesh):
    in_specs = (P("blk", "mp"), P("mp", None), P(("group", "blk", "mp"), None), P("blk"), P(), P())
    out_specs = (
        P(),
        P(),
        P(),
        P("blk", None),
        P(("group", "blk", "mp"), None),
        P("mp", ("group", "blk")),
    )
    return jax.shard_map(
        on_device, mesh=mesh, in_specs=in_specs, out_specs=out_specs, check_vma=False
    )
```
